512 devices in a mesh: cam: 64 (over x_hi, z, core), row: 8 (over y, x_lo).
Axes of the slice: x: 4 (x_hi: 2, x_lo: 2; x = x_hi * 2 + x_lo), y: 4, z: 16, core: 2. Of those that a mesh axis runs over, the one named last changes fastest.
Arguments:
- events: bfloat16 [64, 32, 64, 640], P('cam', None, 'row'), may hold values from -6 to 6
- conv_in: bfloat16 [32, 32, 5, 5], replicated, may hold values from -0.21875 to 0.21875
- bias_in: float32 [32], replicated, may hold values from -3 to 3
- conv_mid: bfloat16 [2, 32, 32, 5, 5], replicated, may hold values from -0.21875 to 0.21875
- bias_mid: float32 [2, 32], replicated, may hold values from -3 to 3
- tap_rows: int32 [2, 48, 64, 4], P(None, None, 'row'), may hold values from 0 to 63, as said below
- tap_weights: float32 [2, 48, 64, 4], P(None, None, 'row'), may hold values from 0 to 1
Outputs:
- volume: bfloat16 [64, 48, 64, 640], P('cam', None, 'row')
- features: bfloat16 [64, 32, 64, 640], P('cam', None, 'row')
The draws below stay inside these ranges and needn't reach their ends.
Inputs may be any that keep to these rules, and one draw needn't show every extreme that they name: tap_rows[d, p, y, k] lies within 4 rows of y and inside the image.
All inputs are finite; a program needn't handle non-finite values.
Results may differ from the reference program's by a relative error of at most 0.0065.
Values may be sent and summed in bfloat16 or wider, within the bound.
A program may use at most 64 MiB of HBM per device.

```python
import jax
import jax.numpy as jnp
from jax import lax

IN_CH = 32
CH = 32
P_SIZE = 48
W_WIN = 640
LAYERS = 3
BAND = 4
TAPS = 4
CAMS = 64
H = 64


def draw_tap_rows(key, part):
    offsets = jax.random.randint(jax.random.fold_in(key, 7), (2, P_SIZE, H, TAPS), -BAND, BAND + 1)
    serving = jnp.arange(H, dtype=jnp.int32)[None, None, :, None]
    return jnp.clip(serving + offsets, 0, H - 1).astype(jnp.int32)


def draw_events(key, part):
    shared_key = jax.random.fold_in(key, 11)
    own_key = jax.random.fold_in(key, 13)
    common = jnp.clip(jax.random.normal(shared_key, (1, IN_CH, H, W_WIN), jnp.float32), -4.0, 4.0)
    single = jnp.clip(jax.random.normal(own_key, (CAMS, IN_CH, H, W_WIN), jnp.float32), -4.0, 4.0)
    return (0.6 * common + 0.8 * single).astype(jnp.bfloat16)


def draw_bias_mid(key, part):
    wide = jnp.clip(0.5 * jax.random.normal(jax.random.fold_in(key, 17), (LAYERS - 1, CH), jnp.float32), -3.0, 3.0)
    narrow = jax.random.uniform(jax.random.fold_in(key, 19), (LAYERS - 1, CH), jnp.float32, -0.05, 0.05)
    last_row = (jnp.arange(LAYERS - 1, dtype=jnp.int32) == LAYERS - 2)[:, None]
    return jnp.where(last_row, narrow, wide).astype(jnp.float32)


def level_of(key, extent, shards, low, top_value):
    level, own = 1.0, jax.random.fold_in(key, 6)
    for position, blocks in shards:
        steps = jnp.exp(jax.random.uniform(jax.random.fold_in(own, position), (blocks,), jnp.float32, low / len(shards), top_value / len(shards)))
        level = level * jnp.repeat(steps, extent[position] // blocks).reshape([-1 if axis == position else 1 for axis in range(len(extent))])
    return level


def gaussian(key, extent, width, most, kind=jnp.bfloat16):
    entries = width * jax.random.normal(key, extent, jnp.float32)
    return jnp.clip(entries, min=-most, max=most).astype(kind)


def setup_inputs(seed: int = 0) -> dict:
    keys = jax.random.split(jax.random.key(seed), 8)
    events = draw_events(jax.random.fold_in(keys[7], 71), 0)
    conv_in = gaussian(keys[1], (CH, IN_CH, 5, 5), (25 * IN_CH) ** -0.5, 0.21875)
    bias_in = gaussian(keys[2], (CH,), 0.5, 3.0, jnp.float32)
    conv_mid = gaussian(keys[3], (LAYERS - 1, CH, CH, 5, 5), (25 * CH) ** -0.5, 0.21875)
    bias_mid = draw_bias_mid(jax.random.fold_in(keys[7], 71), 0)
    tap_rows = draw_tap_rows(jax.random.fold_in(keys[7], 71), 0)
    tap_weights = jnp.clip(1.0 * jax.random.uniform(keys[6], (2, P_SIZE, H, TAPS), jnp.float32) ** level_of(keys[6], (2, P_SIZE, H, TAPS), ((2, 8),), -0.2, 0.2), 0.0, 1.0)
    return dict(events=events, conv_in=conv_in, bias_in=bias_in, conv_mid=conv_mid, bias_mid=bias_mid, tap_rows=tap_rows, tap_weights=tap_weights)


def conv_layer(rows_in, kernel, bias_vec, relu_on, row_pad):
    result = lax.conv_general_dilated(rows_in[None], kernel, (1, 1), ((row_pad, row_pad), (2, 2)), dimension_numbers=("NCHW", "OIHW", "NCHW"), preferred_element_type=jnp.float32)[0]
    result = result + bias_vec[:, None, None]
    if relu_on:
        result = jnp.maximum(result, 0.0)
    return result


def correlate(own_view, partner, tap_rows, tap_weights, first_row):
    row_count = own_view.shape[1]
    span = partner.shape[1] - row_count
    reach = span // 2
    products = []
    for shift_row in range(span + 1):
        window = lax.slice_in_dim(partner, shift_row, shift_row + row_count, axis=1)
        products.append(jnp.einsum("cyx,cyx->yx", own_view, window, preferred_element_type=jnp.float32))
    stacked = jnp.stack(products, axis=1)
    serving = first_row + jnp.arange(row_count, dtype=jnp.int32)
    relative = tap_rows - serving[None, :, None] + reach
    candidate = jnp.arange(span + 1, dtype=jnp.int32)
    weight_table = jnp.sum(tap_weights[..., None] * (relative[..., None] == candidate).astype(jnp.float32), axis=2)
    return jnp.einsum("pyo,yox->pyx", weight_table, stacked, precision=lax.Precision.HIGHEST)


def reference(events, conv_in, bias_in, conv_mid, bias_mid, tap_rows, tap_weights):
    def extract(cam_events):
        current = conv_layer(cam_events, conv_in, bias_in, True, 2).astype(jnp.bfloat16)
        for number in range(LAYERS - 1):
            result = conv_layer(current, conv_mid[number], bias_mid[number], number < LAYERS - 2, 2)
            current = result.astype(jnp.bfloat16)
        return current

    features = lax.map(extract, events)

    def view(camera):
        own_view = lax.dynamic_index_in_dim(features, camera, 0, keepdims=False)
        before = lax.dynamic_index_in_dim(features, (camera + CAMS - 1) % CAMS, 0, keepdims=False)
        later_view = lax.dynamic_index_in_dim(features, (camera + 1) % CAMS, 0, keepdims=False)
        before = jnp.pad(before, ((0, 0), (BAND, BAND), (0, 0)))
        later_view = jnp.pad(later_view, ((0, 0), (BAND, BAND), (0, 0)))
        total = correlate(own_view, before, tap_rows[0], tap_weights[0], 0)
        total = total + correlate(own_view, later_view, tap_rows[1], tap_weights[1], 0)
        return (total / CH).astype(jnp.bfloat16)

    volume = lax.map(view, jnp.arange(CAMS, dtype=jnp.int32))
    return volume, features
```

```python
import functools

import jax
import jax.numpy as jnp
from jax import lax
from jax.experimental import pallas as pl
from jax.experimental.pallas import tpu as pltpu
from jax.sharding import PartitionSpec as P

MESH = pl.DeviceIdType.MESH
F32 = jnp.float32
BF16 = jnp.bfloat16

CH = 32
BANDS = 8
ROWS = 8
COLS = 640
STRIP = COLS // BANDS
HALO = 6
LANES = 128
TILES = COLS // LANES
BLK = CH * ROWS
EDGE = 2 * CH
KROWS = BLK + 2 * EDGE
PLANES = 48
SPAN = 9
REACH = 4
MROWS = 2 * SPAN * ROWS


def lane_ids(shape):
    return lax.broadcasted_iota(jnp.int32, shape, 1)


def row_ids(shape):
    return lax.broadcasted_iota(jnp.int32, shape, 0)


def roll(value, shift):
    shift = shift % value.shape[1]
    return value if shift == 0 else pltpu.roll(value, shift, 1)


def row_major_perm():
    shape = (BLK, BLK)
    i, j = row_ids(shape), lane_ids(shape)
    return ((i & 31) * ROWS + (i >> 5) == j).astype(BF16)


def channel_major_perm():
    shape = (BLK, BLK)
    i, j = row_ids(shape), lane_ids(shape)
    return ((i & 7) * CH + (i >> 3) == j).astype(BF16)


def window_of(tiles, strip):
    start = STRIP * strip - HALO
    first = start // LANES
    off = start - first * LANES
    shape = tiles[0].shape
    low = roll(tiles[first], -off) if first >= 0 else jnp.zeros(shape, F32)
    if LANES - off >= STRIP + 2 * HALO:
        return low
    high = roll(tiles[first + 1], -off) if first + 1 < TILES else jnp.zeros(shape, F32)
    return jnp.where(lane_ids(shape) < LANES - off, low, high)


def unwindow(get, tile):
    out = None
    for strip in range(BANDS):
        lo = max(STRIP * strip, LANES * tile) - LANES * tile
        hi = min(STRIP * (strip + 1), LANES * (tile + 1)) - LANES * tile
        if lo < hi:
            value = roll(get(strip), STRIP * strip - HALO - LANES * tile)
            out = value if out is None else jnp.where(lane_ids(value.shape) >= lo, value, out)
    return out


def build_taps(w, t_ref):
    for dx in range(5):
        pieces = [w(dy, dx).astype(F32) for dy in range(5)]
        base = jnp.concatenate(pieces + [jnp.zeros((CH, KROWS - 5 * CH), F32)], axis=1)
        for y in range(ROWS):
            t_ref[CH * y : CH * (y + 1), KROWS * dx : KROWS * (dx + 1)] = roll(base, CH * y).astype(BF16)


def bias_column(bias_row, channel_major):
    shape = (BLK, CH)
    i = row_ids(shape)
    owner = (i >> 3) if channel_major else (i & 31)
    spread = jnp.where(owner == lane_ids(shape), jnp.broadcast_to(bias_row, shape), 0.0)
    return jnp.broadcast_to(jnp.sum(spread, axis=1, keepdims=True), (BLK, LANES))


def kernel(
    cams,
    ev_ref, w1_ref, wm_ref, b1_ref, bm_ref, rows_ref, wts_ref,
    vol_ref, feat_ref,
    win, x1, x2, x3, t1, t2, t3, bias, fblk, frx, fown, fpart, fback, macc, msend, mrecv, tab,
    s1_send, s1_recv, f_send, f_recv, o_send, o_recv, m_send, m_recv,
):
    cam = lax.axis_index("cam")
    me = lax.axis_index("row")
    nxt = (lax.rem(cam + 1, cams), me)
    prv = (lax.rem(cam + cams - 1, cams), me)
    peers = [lax.rem(me + k, BANDS) for k in range(1, BANDS)]

    barrier = pltpu.get_barrier_semaphore()
    for peer in peers:
        pl.semaphore_signal(barrier, inc=1, device_id=(cam, peer), device_id_type=MESH)
    for peer in (nxt, prv):
        pl.semaphore_signal(barrier, inc=1, device_id=peer, device_id_type=MESH)

    ev = jnp.dot(row_major_perm(), ev_ref[...], preferred_element_type=F32)
    tiles = [ev[:, LANES * t : LANES * (t + 1)] for t in range(TILES)]
    for strip in range(BANDS):
        win[strip] = window_of(tiles, strip).astype(BF16)

    pl.semaphore_wait(barrier, BANDS + 1)

    def block_rows(b):
        return pl.ds(pl.multiple_of(EDGE + b * BLK, EDGE), BLK)

    def s1_copy(dst, src_row):
        return pltpu.make_async_remote_copy(
            src_ref=win.at[dst],
            dst_ref=x1.at[block_rows(src_row)],
            send_sem=s1_send.at[dst],
            recv_sem=s1_recv.at[src_row],
            device_id=(cam, dst),
            device_id_type=MESH,
        )

    for peer in peers:
        s1_copy(peer, me).start()
    x1[block_rows(me)] = win[me]

    zero_edge = jnp.zeros((EDGE, LANES), BF16)
    for x in (x1, x2, x3):
        x[0:EDGE] = zero_edge
        x[EDGE + BANDS * BLK :] = zero_edge
    build_taps(lambda dy, dx: w1_ref[dy, dx], t1)
    build_taps(lambda dy, dx: wm_ref[0, dy, dx], t2)
    build_taps(lambda dy, dx: wm_ref[1, dy, dx], t3)
    perm = channel_major_perm()
    for dx in range(5):
        cols = slice(KROWS * dx, KROWS * (dx + 1))
        t3[:, cols] = jnp.dot(perm, t3[:, cols], preferred_element_type=F32).astype(BF16)
    bias[0] = bias_column(b1_ref[...], False)
    bias[1] = bias_column(bm_ref[0:1], False)
    bias[2] = bias_column(bm_ref[1:2], True)
    for d in range(2):
        fpart[d, :, 0:ROWS] = jnp.zeros((CH, ROWS, LANES), F32)
        fpart[d, :, ROWS * (BANDS + 1) :] = jnp.zeros((CH, ROWS, LANES), F32)

    first = me * ROWS
    shape = (ROWS, LANES)
    pick = (
        ((row_ids((PLANES * ROWS, 4 * LANES)) & 7) * 64 + (row_ids((PLANES * ROWS, 4 * LANES)) >> 3))
        == lane_ids((PLANES * ROWS, 4 * LANES))
    ).astype(BF16)
    serving = first + row_ids((ROWS, PLANES)) - REACH
    parts = []
    for d in range(2):
        for o in range(SPAN):
            total = jnp.zeros((ROWS, PLANES), F32)
            for k in range(4):
                hit = rows_ref[d, :, k] == serving + o
                total = total + jnp.where(hit, wts_ref[d, :, k], 0.0)
            total = total * (1.0 / CH)
            wide = jnp.concatenate([total, jnp.zeros((ROWS, 64 - PLANES), F32)], axis=1)
            wide = jnp.concatenate([wide, wide], axis=1)
            half = lane_ids(shape) >> 6
            parts.append(
                jnp.concatenate(
                    [jnp.where(row_ids(shape) == 2 * j + half, wide, 0.0) for j in range(4)], axis=1
                )
            )
    table = jnp.concatenate(parts, axis=0)
    high = table.astype(BF16)
    low = (table - high.astype(F32)).astype(BF16)
    for n, piece in enumerate((high, low)):
        tab[n] = lax.dot_general(
            pick, piece, (((1,), (1,)), ((), ())), preferred_element_type=F32
        ).astype(BF16)

    for k in range(1, BANDS):
        s1_copy(peers[0], lax.rem(me + BANDS - k, BANDS)).wait_recv()

    column = lane_ids((1, LANES)) + me * STRIP - HALO
    inside = jnp.logical_and(column >= 0, column < COLS)

    def conv(x, t, pair):
        halves = []
        for b in (2 * pair, 2 * pair + 1):
            rows = x[BLK * b : BLK * b + KROWS].astype(F32)
            halves.append(
                jnp.concatenate([roll(rows, 2 - dx).astype(BF16) for dx in range(5)], axis=0)
            )
        return jnp.dot(t[...], jnp.concatenate(halves, axis=1), preferred_element_type=F32)

    def hidden(x, t, number, y, pair):
        out = conv(x, t, pair)
        for h in range(2):
            value = jnp.maximum(out[:, LANES * h : LANES * (h + 1)] + bias[number], 0.0)
            start = EDGE + BLK * (2 * pair + h)
            y[start : start + BLK] = jnp.where(inside, value, 0.0).astype(BF16)

    def f_copy(d, b):
        return pltpu.make_async_remote_copy(
            src_ref=fblk.at[b],
            dst_ref=frx.at[d, b],
            send_sem=f_send.at[d, b],
            recv_sem=f_recv.at[d, b],
            device_id=nxt if d == 0 else prv,
            device_id_type=MESH,
        )

    def last(pair):
        out = conv(x3, t3, pair)
        for h in range(2):
            b = 2 * pair + h
            value = (out[:, LANES * h : LANES * (h + 1)] + bias[2]).astype(BF16)
            fblk[b] = value
            fown[:, ROWS * b : ROWS * (b + 1)] = value.astype(F32).reshape(CH, ROWS, LANES)
            for d in range(2):
                f_copy(d, b).start()

    pairs = BANDS // 2
    for step in range(pairs + 2):
        if step < pairs:
            hidden(x1, t1, 0, x2, step)
        if 0 <= step - 1 < pairs:
            hidden(x2, t2, 1, x3, step - 1)
        if 0 <= step - 2 < pairs:
            last(step - 2)

    def o_copy(dst, strip):
        return pltpu.make_async_remote_copy(
            src_ref=fblk.at[dst],
            dst_ref=fback.at[strip],
            send_sem=o_send.at[dst],
            recv_sem=o_recv.at[strip],
            device_id=(cam, dst),
            device_id_type=MESH,
        )

    for peer in peers:
        o_copy(peer, me).start()
    fback[me] = fblk[me]

    def m_copy(dst, strip):
        return pltpu.make_async_remote_copy(
            src_ref=msend.at[dst],
            dst_ref=mrecv.at[strip],
            send_sem=m_send.at[dst],
            recv_sem=m_recv.at[strip],
            device_id=(cam, dst),
            device_id_type=MESH,
        )

    def arrive(b):
        for d in range(2):
            f_copy(d, b).wait_recv()
            fpart[d, :, ROWS * (b + 1) : ROWS * (b + 2)] = (
                frx[d, b].astype(F32).reshape(CH, ROWS, LANES)
            )

    def match(b):
        for d in range(2):

            def channel(c, acc):
                own = fown[c, ROWS * b : ROWS * (b + 1)]
                return tuple(
                    acc[o] + own * fpart[d, c, ROWS * (b + 1) + o - REACH : ROWS * (b + 2) + o - REACH]
                    for o in range(SPAN)
                )

            acc = lax.fori_loop(
                0, CH, channel, tuple(jnp.zeros((ROWS, LANES), F32) for _ in range(SPAN)), unroll=8
            )
            for o in range(SPAN):
                start = (d * SPAN + o) * ROWS
                macc[start : start + ROWS] = acc[o]
        msend[b] = macc[...].astype(BF16)

        @pl.when(me != b)
        def _():
            m_copy(b, me).start()

    arrive(0)
    for b in range(BANDS):
        if b + 1 < BANDS:
            arrive(b + 1)
        match(b)
    mrecv[me] = msend[me]

    for k in range(1, BANDS):
        o_copy(peers[0], lax.rem(me + BANDS - k, BANDS)).wait_recv()
    for t in range(TILES):
        feat_ref[:, LANES * t : LANES * (t + 1)] = unwindow(
            lambda s: fback[s].astype(F32), t
        ).astype(BF16)

    for k in range(1, BANDS):
        m_copy(peers[0], lax.rem(me + BANDS - k, BANDS)).wait_recv()
    for t in range(TILES):
        values = unwindow(lambda s: mrecv[s].astype(F32), t).astype(BF16)
        out = jnp.dot(tab[0], values, preferred_element_type=F32)
        out = out + jnp.dot(tab[1], values, preferred_element_type=F32)
        vol_ref[:, LANES * t : LANES * (t + 1)] = out.astype(BF16)

    for peer in peers:
        s1_copy(peer, me).wait_send()
        o_copy(peer, me).wait_send()
        m_copy(peer, me).wait_send()
    for b in range(BANDS):
        for d in range(2):
            f_copy(d, b).wait_send()


def local(cams, events, conv_in, bias_in, conv_mid, bias_mid, tap_rows, tap_weights):
    dma = pltpu.SemaphoreType.DMA
    vmem = pl.BlockSpec(memory_space=pltpu.VMEM)
    padded = (BANDS * BLK + 2 * EDGE, LANES)
    taps = (BLK, 5 * KROWS)
    vol, feat = pl.pallas_call(
        functools.partial(kernel, cams),
        out_shape=(
            jax.ShapeDtypeStruct((PLANES * ROWS, COLS), BF16),
            jax.ShapeDtypeStruct((BLK, COLS), BF16),
        ),
        in_specs=[vmem] * 7,
        out_specs=(vmem, vmem),
        scratch_shapes=[
            pltpu.VMEM((BANDS, BLK, LANES), BF16),
            pltpu.VMEM(padded, BF16),
            pltpu.VMEM(padded, BF16),
            pltpu.VMEM(padded, BF16),
            pltpu.VMEM(taps, BF16),
            pltpu.VMEM(taps, BF16),
            pltpu.VMEM(taps, BF16),
            pltpu.VMEM((3, BLK, LANES), F32),
            pltpu.VMEM((BANDS, BLK, LANES), BF16),
            pltpu.VMEM((2, BANDS, BLK, LANES), BF16),
            pltpu.VMEM((CH, ROWS * BANDS, LANES), F32),
            pltpu.VMEM((2, CH, ROWS * (BANDS + 2), LANES), F32),
            pltpu.VMEM((BANDS, BLK, LANES), BF16),
            pltpu.VMEM((MROWS, LANES), F32),
            pltpu.VMEM((BANDS, MROWS, LANES), BF16),
            pltpu.VMEM((BANDS, MROWS, LANES), BF16),
            pltpu.VMEM((2, PLANES * ROWS, MROWS), BF16),
            dma((BANDS,)), dma((BANDS,)),
            dma((2, BANDS)), dma((2, BANDS)),
            dma((BANDS,)), dma((BANDS,)),
            dma((BANDS,)), dma((BANDS,)),
        ],
        compiler_params=pltpu.CompilerParams(
            collective_id=0, has_side_effects=True, vmem_limit_bytes=40 * 1024 * 1024
        ),
    )(
        events.reshape(BLK, COLS),
        conv_in.transpose(2, 3, 0, 1),
        conv_mid.transpose(0, 3, 4, 1, 2),
        bias_in.reshape(1, CH),
        bias_mid,
        tap_rows.transpose(0, 2, 3, 1),
        tap_weights.transpose(0, 2, 3, 1),
    )
    return vol.reshape(1, PLANES, ROWS, COLS), feat.reshape(1, CH, ROWS, COLS)


def solution(mesh):
    in_specs = (
        P("cam", None, "row", None),
        P(),
        P(),
        P(),
        P(),
        P(None, None, "row", None),
        P(None, None, "row", None),
    )
    out_specs = (P("cam", None, "row", None), P("cam", None, "row", None))
    return jax.shard_map(
        functools.partial(local, mesh.shape["cam"]),
        mesh=mesh,
        in_specs=in_specs,
        out_specs=out_specs,
        check_vma=False,
    )
```

```python
import functools

import jax
import jax.numpy as jnp
from jax import lax
from jax.experimental import pallas as pl
from jax.experimental.pallas import tpu as pltpu
from jax.sharding import PartitionSpec as P

MESH = pl.DeviceIdType.MESH
F32 = jnp.float32
BF16 = jnp.bfloat16

CH = 32
BANDS = 8
ROWS = 8
COLS = 640
STRIP = COLS // BANDS
HALO = 6
LANES = 128
TILES = COLS // LANES
BLK = CH * ROWS
EDGE = 2 * CH
KROWS = BLK + 2 * EDGE
PLANES = 48
SPAN = 9
REACH = 4
MROWS = SPAN * ROWS
GROUPS = 4
PACK = 5
FROWS = GROUPS * PACK * ROWS
MPACK = 6 * ROWS


def lane_ids(shape):
    return lax.broadcasted_iota(jnp.int32, shape, 1)


def row_ids(shape):
    return lax.broadcasted_iota(jnp.int32, shape, 0)


def roll(value, shift):
    shift = shift % value.shape[1]
    return value if shift == 0 else pltpu.roll(value, shift, 1)


def row_major_perm():
    shape = (BLK, BLK)
    i, j = row_ids(shape), lane_ids(shape)
    return ((i & 31) * ROWS + (i >> 5) == j).astype(BF16)


def channel_major_perm():
    shape = (BLK, BLK)
    i, j = row_ids(shape), lane_ids(shape)
    return ((i & 7) * CH + (i >> 3) == j).astype(BF16)


def window_of(tiles, strip):
    start = STRIP * strip - HALO
    first = start // LANES
    off = start - first * LANES
    shape = tiles[0].shape
    low = roll(tiles[first], -off) if first >= 0 else jnp.zeros(shape, F32)
    if LANES - off >= STRIP + 2 * HALO:
        return low
    high = roll(tiles[first + 1], -off) if first + 1 < TILES else jnp.zeros(shape, F32)
    return jnp.where(lane_ids(shape) < LANES - off, low, high)


def place(pieces, tile):
    out = None
    for get, lane, column, count in pieces:
        lo = max(column, LANES * tile) - LANES * tile
        hi = min(column + count, LANES * (tile + 1)) - LANES * tile
        if lo < hi:
            value = roll(get(), column - LANES * tile - lane)
            out = value if out is None else jnp.where(lane_ids(value.shape) >= lo, value, out)
    return out


def pack_features(value):
    lane = lane_ids((ROWS, LANES))
    out = []
    for g in range(GROUPS):
        tail = None
        for k in range(4):
            even = roll(value[8 * g + 2 * k], -HALO)
            odd = roll(value[8 * g + 2 * k + 1], 64 - HALO)
            out.append(jnp.where(lane < 64, even, odd))
            both = roll(jnp.where(lane < 64, odd, even), 16 * k)
            tail = both if tail is None else jnp.where((lane & 63) >= 16 * k, both, tail)
        out.append(tail)
    return out


def build_taps(w, t_ref):
    for dx in range(5):
        pieces = [w(dy, dx).astype(F32) for dy in range(5)]
        base = jnp.concatenate(pieces + [jnp.zeros((CH, KROWS - 5 * CH), F32)], axis=1)
        for y in range(ROWS):
            t_ref[CH * y : CH * (y + 1), KROWS * dx : KROWS * (dx + 1)] = roll(base, CH * y).astype(BF16)


def bias_column(bias_row, channel_major):
    shape = (BLK, CH)
    i = row_ids(shape)
    owner = (i >> 3) if channel_major else (i & 31)
    spread = jnp.where(owner == lane_ids(shape), jnp.broadcast_to(bias_row, shape), 0.0)
    return jnp.broadcast_to(jnp.sum(spread, axis=1, keepdims=True), (BLK, LANES))


def kernel(
    cams,
    ev_hbm, w1_hbm, wm_hbm, b1_hbm, bm_hbm, rows_hbm, wts_hbm,
    vol_ref, feat_ref,
    ev_ref, w1_ref, wm_ref, b1_ref, bm_ref, rows_ref, wts_ref,
    win, x1, x2, x3, t1, t2, t3, bias, fblk, frx, fown, fpart, fback, msend, mrecv, mval, featf, wide, tab,
    in_sem, s1_send, s1_recv, f_send, f_recv, o_send, o_recv, m_send, m_recv,
):
    cam = lax.axis_index("cam")
    me = lax.axis_index("row")
    odd = lax.rem(cam, 2)
    far = (lax.rem(cam + cams - 1 + 2 * odd, cams), me)
    near = (cam + 1 - 2 * odd, me)
    peers = [lax.rem(me + k, BANDS) for k in range(1, BANDS)]

    barrier = pltpu.get_barrier_semaphore()
    for peer in peers:
        pl.semaphore_signal(barrier, inc=1, device_id=(cam, peer), device_id_type=MESH)
    for peer in (far, near):
        pl.semaphore_signal(barrier, inc=1, device_id=peer, device_id_type=MESH)
    loads = [
        pltpu.make_async_copy(src, dst, in_sem.at[n])
        for n, (src, dst) in enumerate(
            (
                (ev_hbm, ev_ref), (w1_hbm, w1_ref), (wm_hbm, wm_ref), (b1_hbm, b1_ref),
                (bm_hbm, bm_ref), (rows_hbm, rows_ref), (wts_hbm, wts_ref),
            )
        )
    ]
    for load in loads:
        load.start()
    loads[0].wait()

    ev = jnp.dot(row_major_perm(), ev_ref[...], preferred_element_type=F32)
    tiles = [ev[:, LANES * t : LANES * (t + 1)] for t in range(TILES)]
    for strip in range(BANDS):
        win[strip] = window_of(tiles, strip).astype(BF16)

    pl.semaphore_wait(barrier, BANDS + 1)

    def block_rows(b):
        return pl.ds(pl.multiple_of(EDGE + b * BLK, EDGE), BLK)

    def s1_copy(dst, src_row):
        return pltpu.make_async_remote_copy(
            src_ref=win.at[dst],
            dst_ref=x1.at[block_rows(src_row)],
            send_sem=s1_send.at[dst],
            recv_sem=s1_recv.at[src_row],
            device_id=(cam, dst),
            device_id_type=MESH,
        )

    for peer in peers:
        s1_copy(peer, me).start()
    x1[block_rows(me)] = win[me]

    for load in loads[1:]:
        load.wait()

    zero_edge = jnp.zeros((EDGE, LANES), BF16)
    for x in (x1, x2, x3):
        x[0:EDGE] = zero_edge
        x[EDGE + BANDS * BLK :] = zero_edge
    build_taps(lambda dy, dx: w1_ref[dy, dx], t1)
    build_taps(lambda dy, dx: wm_ref[0, dy, dx], t2)
    build_taps(lambda dy, dx: wm_ref[1, dy, dx], t3)
    perm = channel_major_perm()
    for dx in range(5):
        cols = slice(KROWS * dx, KROWS * (dx + 1))
        t3[:, cols] = jnp.dot(perm, t3[:, cols], preferred_element_type=F32).astype(BF16)
    bias[0] = bias_column(b1_ref[...], False)
    bias[1] = bias_column(bm_ref[0:1], False)
    bias[2] = bias_column(bm_ref[1:2], True)
    for d in range(2):
        edge = jnp.zeros((GROUPS * PACK, ROWS, LANES), F32)
        fpart[d, :, 0:ROWS] = edge
        fpart[d, :, ROWS * (BANDS + 1) :] = edge

    first = me * ROWS
    shape = (ROWS, LANES)
    pick = (
        ((row_ids((PLANES * ROWS, 4 * LANES)) & 7) * 64 + (row_ids((PLANES * ROWS, 4 * LANES)) >> 3))
        == lane_ids((PLANES * ROWS, 4 * LANES))
    ).astype(BF16)
    serving = first + row_ids((ROWS, PLANES)) - REACH
    parts = []
    for kind in range(2):
        d = odd if kind == 0 else 1 - odd
        for o in range(SPAN):
            total = jnp.zeros((ROWS, PLANES), F32)
            for k in range(4):
                hit = rows_ref[d, :, k] == serving + o
                total = total + jnp.where(hit, wts_ref[d, :, k], 0.0)
            total = total * (1.0 / CH)
            doubled = jnp.concatenate([total, jnp.zeros((ROWS, 64 - PLANES), F32)], axis=1)
            doubled = jnp.concatenate([doubled, doubled], axis=1)
            half = lane_ids(shape) >> 6
            parts.append(
                jnp.concatenate(
                    [jnp.where(row_ids(shape) == 2 * j + half, doubled, 0.0) for j in range(4)], axis=1
                )
            )
    table = jnp.concatenate(parts, axis=0)
    high = table.astype(BF16)
    low = (table - high.astype(F32)).astype(BF16)
    for n, piece in enumerate((high, low)):
        tab[n] = lax.dot_general(
            pick, piece, (((1,), (1,)), ((), ())), preferred_element_type=F32
        ).astype(BF16)

    for k in range(1, BANDS):
        s1_copy(peers[0], lax.rem(me + BANDS - k, BANDS)).wait_recv()

    column = lane_ids((1, LANES)) + me * STRIP - HALO
    inside = jnp.logical_and(column >= 0, column < COLS)

    def conv(x, t, pair):
        halves = []
        for b in (2 * pair, 2 * pair + 1):
            rows = x[BLK * b : BLK * b + KROWS].astype(F32)
            halves.append(
                jnp.concatenate([roll(rows, 2 - dx).astype(BF16) for dx in range(5)], axis=0)
            )
        return jnp.dot(t[...], jnp.concatenate(halves, axis=1), preferred_element_type=F32)

    def hidden(x, t, number, y, pair):
        out = conv(x, t, pair)
        for h in range(2):
            value = jnp.maximum(out[:, LANES * h : LANES * (h + 1)] + bias[number], 0.0)
            start = EDGE + BLK * (2 * pair + h)
            y[start : start + BLK] = jnp.where(inside, value, 0.0).astype(BF16)

    def f_copy(kind, b):
        return pltpu.make_async_remote_copy(
            src_ref=fblk.at[b],
            dst_ref=frx.at[kind, b],
            send_sem=f_send.at[kind, b],
            recv_sem=f_recv.at[kind, b],
            device_id=far if kind == 0 else near,
            device_id_type=MESH,
        )

    def o_copy(dst, strip):
        return pltpu.make_async_remote_copy(
            src_ref=fblk.at[dst],
            dst_ref=fback.at[strip],
            send_sem=o_send.at[dst],
            recv_sem=o_recv.at[strip],
            device_id=(cam, dst),
            device_id_type=MESH,
        )

    def last(pair):
        out = conv(x3, t3, pair)
        for h in range(2):
            b = 2 * pair + h
            value = out[:, LANES * h : LANES * (h + 1)] + bias[2]
            packed = jnp.concatenate(pack_features(value.reshape(CH, ROWS, LANES)), axis=0)
            packed = packed.astype(BF16)
            fblk[b] = packed
            fown[:, ROWS * b : ROWS * (b + 1)] = packed.astype(F32).reshape(GROUPS * PACK, ROWS, LANES)
            for kind in range(2):
                f_copy(kind, b).start()

            @pl.when(me != b)
            def _():
                o_copy(b, me).start()

    pairs = BANDS // 2
    for step in range(pairs + 2):
        if step < pairs:
            hidden(x1, t1, 0, x2, step)
        if 0 <= step - 1 < pairs:
            hidden(x2, t2, 1, x3, step - 1)
        if 0 <= step - 2 < pairs:
            last(step - 2)

    fback[me] = fblk[me]

    def m_copy(kind, dst, strip):
        return pltpu.make_async_remote_copy(
            src_ref=msend.at[kind, dst],
            dst_ref=mrecv.at[kind, strip],
            send_sem=m_send.at[kind, dst],
            recv_sem=m_recv.at[kind, strip],
            device_id=(cam, dst),
            device_id_type=MESH,
        )

    def arrive(kind, b):
        f_copy(kind, b).wait_recv()
        fpart[kind, :, ROWS * (b + 1) : ROWS * (b + 2)] = (
            frx[kind, b].astype(F32).reshape(GROUPS * PACK, ROWS, LANES)
        )

    lane = lane_ids((ROWS, LANES))

    def match(kind, b):
        def products(n, acc):
            own = fown[n, ROWS * b : ROWS * (b + 1)]
            return tuple(
                acc[o] + own * fpart[kind, n, ROWS * (b + 1) + o - REACH : ROWS * (b + 2) + o - REACH]
                for o in range(SPAN)
            )

        def group(g, accs):
            main, tail = accs
            for k in range(4):
                main = products(PACK * g + k, main)
            return main, products(PACK * g + 4, tail)

        zeros = tuple(jnp.zeros((ROWS, LANES), F32) for _ in range(SPAN))
        main, tail = lax.fori_loop(0, GROUPS, group, (zeros, zeros), unroll=2)
        main = [v + roll(v, 64) for v in main]
        for step in (64, 32, 16):
            tail = [v + roll(v, step) for v in tail]
        out = [jnp.where(lane < 64, main[2 * k], main[2 * k + 1]) for k in range(4)]
        ends = tail[0]
        for o in range(1, 8):
            ends = jnp.where(lane >= 16 * o, tail[o], ends)
        out.append(ends)
        out.append(jnp.where(lane < 64, main[8], tail[8]))
        msend[kind, b] = jnp.concatenate(out, axis=0).astype(BF16)

        @pl.when(me != b)
        def _():
            m_copy(kind, b, me).start()

    for kind in (1, 0):
        arrive(kind, 0)
        for b in range(BANDS):
            if b + 1 < BANDS:
                arrive(kind, b + 1)
            match(kind, b)
        mrecv[kind, me] = msend[kind, me]

    for k in range(1, BANDS):
        o_copy(peers[0], lax.rem(me + BANDS - k, BANDS)).wait_recv()
    for c in range(CH):
        g, k, h = c >> 3, (c & 7) >> 1, c & 1
        body = (PACK * g + k) * ROWS
        ends = (PACK * g + 4) * ROWS
        end_lane = 16 * k if h else 64 + 16 * k
        pieces = []
        for s in range(BANDS):
            pieces.append((lambda s=s: wide[s, body : body + ROWS], 64 * h, STRIP * s, 64))
            pieces.append((lambda s=s: wide[s, ends : ends + ROWS], end_lane, STRIP * s + 64, 16))
        if c == 0:
            for s in range(BANDS):
                wide[s] = fback[s].astype(F32)
        for t in range(TILES):
            featf[ROWS * c : ROWS * (c + 1), LANES * t : LANES * (t + 1)] = place(pieces, t)
    feat_ref[...] = featf[...].astype(BF16)

    for kind in (1, 0):
        for k in range(1, BANDS):
            m_copy(kind, peers[0], lax.rem(me + BANDS - k, BANDS)).wait_recv()
        for s in range(BANDS):
            wide[s, 0:MPACK] = mrecv[kind, s].astype(F32)
        for o in range(SPAN):
            body = 8 * (o >> 1) if o < 8 else 5 * ROWS
            body_lane = 64 * (o & 1) if o < 8 else 0
            ends = 4 * ROWS if o < 8 else 5 * ROWS
            end_lane = 16 * o if o < 8 else 64
            pieces = []
            for s in range(BANDS):
                pieces.append((lambda s=s: wide[s, body : body + ROWS], body_lane, STRIP * s, 64))
                pieces.append((lambda s=s: wide[s, ends : ends + ROWS], end_lane, STRIP * s + 64, 16))
            start = MROWS * kind + ROWS * o
            for t in range(TILES):
                mval[start : start + ROWS, LANES * t : LANES * (t + 1)] = place(pieces, t)
    values = mval[...].astype(BF16)
    out = jnp.dot(tab[0], values, preferred_element_type=F32)
    out = out + jnp.dot(tab[1], values, preferred_element_type=F32)
    vol_ref[...] = out.astype(BF16)

    for peer in peers:
        s1_copy(peer, me).wait_send()
        o_copy(peer, me).wait_send()
        for kind in range(2):
            m_copy(kind, peer, me).wait_send()
    for b in range(BANDS):
        for kind in range(2):
            f_copy(kind, b).wait_send()


def local(cams, events, conv_in, bias_in, conv_mid, bias_mid, tap_rows, tap_weights):
    dma = pltpu.SemaphoreType.DMA
    vmem = pl.BlockSpec(memory_space=pltpu.VMEM)
    padded = (BANDS * BLK + 2 * EDGE, LANES)
    taps = (BLK, 5 * KROWS)
    operands = (
        events.reshape(BLK, COLS),
        conv_in.transpose(2, 3, 0, 1),
        conv_mid.transpose(0, 3, 4, 1, 2),
        bias_in.reshape(1, CH),
        bias_mid,
        tap_rows.transpose(0, 2, 3, 1),
        tap_weights.transpose(0, 2, 3, 1),
    )
    vol, feat = pl.pallas_call(
        functools.partial(kernel, cams),
        out_shape=(
            jax.ShapeDtypeStruct((PLANES * ROWS, COLS), BF16),
            jax.ShapeDtypeStruct((BLK, COLS), BF16),
        ),
        in_specs=[pl.BlockSpec(memory_space=pltpu.HBM)] * 7,
        out_specs=(vmem, vmem),
        scratch_shapes=[
            *[pltpu.VMEM(operand.shape, operand.dtype) for operand in operands],
            pltpu.VMEM((BANDS, BLK, LANES), BF16),
            pltpu.VMEM(padded, BF16),
            pltpu.VMEM(padded, BF16),
            pltpu.VMEM(padded, BF16),
            pltpu.VMEM(taps, BF16),
            pltpu.VMEM(taps, BF16),
            pltpu.VMEM(taps, BF16),
            pltpu.VMEM((3, BLK, LANES), F32),
            pltpu.VMEM((BANDS, FROWS, LANES), BF16),
            pltpu.VMEM((2, BANDS, FROWS, LANES), BF16),
            pltpu.VMEM((GROUPS * PACK, ROWS * BANDS, LANES), F32),
            pltpu.VMEM((2, GROUPS * PACK, ROWS * (BANDS + 2), LANES), F32),
            pltpu.VMEM((BANDS, FROWS, LANES), BF16),
            pltpu.VMEM((2, BANDS, MPACK, LANES), BF16),
            pltpu.VMEM((2, BANDS, MPACK, LANES), BF16),
            pltpu.VMEM((2 * MROWS, COLS), F32),
            pltpu.VMEM((BLK, COLS), F32),
            pltpu.VMEM((BANDS, FROWS, LANES), F32),
            pltpu.VMEM((2, PLANES * ROWS, 2 * MROWS), BF16),
            dma((7,)),
            dma((BANDS,)), dma((BANDS,)),
            dma((2, BANDS)), dma((2, BANDS)),
            dma((BANDS,)), dma((BANDS,)),
            dma((2, BANDS)), dma((2, BANDS)),
        ],
        compiler_params=pltpu.CompilerParams(
            collective_id=0, has_side_effects=True, vmem_limit_bytes=64 * 1024 * 1024
        ),
    )(*operands)
    return vol.reshape(1, PLANES, ROWS, COLS), feat.reshape(1, CH, ROWS, COLS)


def solution(mesh):
    in_specs = (
        P("cam", None, "row", None),
        P(),
        P(),
        P(),
        P(),
        P(None, None, "row", None),
        P(None, None, "row", None),
    )
    out_specs = (P("cam", None, "row", None), P("cam", None, "row", None))
    return jax.shard_map(
        functools.partial(local, mesh.shape["cam"]),
        mesh=mesh,
        in_specs=in_specs,
        out_specs=out_specs,
        check_vma=False,
    )
```

```python
import functools

import jax
import jax.numpy as jnp
from jax import lax
from jax.experimental import pallas as pl
from jax.experimental.pallas import tpu as pltpu
from jax.sharding import PartitionSpec as P

MESH = pl.DeviceIdType.MESH
F32 = jnp.float32
BF16 = jnp.bfloat16

CH = 32
BANDS = 8
ROWS = 8
COLS = 640
STRIP = COLS // BANDS
HALO = 6
LANES = 128
TILES = COLS // LANES
BLK = CH * ROWS
EDGE = 2 * CH
KROWS = BLK + 2 * EDGE
PLANES = 48
SPAN = 9
REACH = 4
MROWS = SPAN * ROWS
GROUPS = 4
PACK = 5
FROWS = GROUPS * PACK * ROWS
MPACK = 6 * ROWS
QUARTER = BLK // 4
WROWS = 3 * QUARTER


def lane_ids(shape):
    return lax.broadcasted_iota(jnp.int32, shape, 1)


def row_ids(shape):
    return lax.broadcasted_iota(jnp.int32, shape, 0)


def roll(value, shift):
    shift = shift % value.shape[1]
    return value if shift == 0 else pltpu.roll(value, shift, 1)


def row_major_perm():
    shape = (BLK, BLK)
    i, j = row_ids(shape), lane_ids(shape)
    return ((i & 31) * ROWS + (i >> 5) == j).astype(BF16)


def channel_major_perm():
    shape = (BLK, BLK)
    i, j = row_ids(shape), lane_ids(shape)
    return ((i & 7) * CH + (i >> 3) == j).astype(BF16)


def window_of(tiles, strip):
    start = STRIP * strip - HALO
    first = start // LANES
    off = start - first * LANES
    shape = tiles[0].shape
    low = roll(tiles[first], -off) if first >= 0 else jnp.zeros(shape, BF16)
    if LANES - off >= STRIP + 2 * HALO:
        return low
    high = roll(tiles[first + 1], -off) if first + 1 < TILES else jnp.zeros(shape, BF16)
    return jnp.where(lane_ids(shape) < LANES - off, low, high)


def pack_window(value):
    lane = lane_ids((QUARTER, LANES))
    parts = [value[QUARTER * g : QUARTER * (g + 1)] for g in range(4)]
    pairs = [jnp.where(lane < 64, parts[g], roll(parts[g + 1], 64)) for g in (0, 2)]
    tail = roll(parts[0], -64)
    for g in range(1, 4):
        tail = jnp.where(lane >= 32 * g, roll(parts[g], 32 * g - 64), tail)
    return jnp.concatenate(pairs + [tail], axis=0)


def unpack_window(packed):
    lane = lane_ids((QUARTER, LANES))
    tail = packed[2 * QUARTER :]
    parts = []
    for g in range(4):
        pair = packed[QUARTER * (g // 2) : QUARTER * (g // 2 + 1)]
        parts.append(jnp.where(lane < 64, roll(pair, 64 * (g & 1)), roll(tail, 64 - 32 * g)))
    return jnp.concatenate(parts, axis=0)


def fold(lane, step, even, odd):
    clear = (lane & step) == 0
    own = jnp.where(clear, even, odd)
    other = jnp.where(clear, odd, even)
    if step == 64:
        return own + roll(other, 64)
    return own + jnp.where(clear, roll(other, -step), roll(other, step))


def place(pieces, tile):
    out = None
    for get, lane, column, count in pieces:
        lo = max(column, LANES * tile) - LANES * tile
        hi = min(column + count, LANES * (tile + 1)) - LANES * tile
        if lo < hi:
            value = roll(get(), column - LANES * tile - lane)
            out = value if out is None else jnp.where(lane_ids(value.shape) >= lo, value, out)
    return out


def pack_features(value):
    lane = lane_ids((ROWS, LANES))
    out = []
    for g in range(GROUPS):
        tail = None
        for k in range(4):
            even = roll(value[8 * g + 2 * k], -HALO)
            odd = roll(value[8 * g + 2 * k + 1], 64 - HALO)
            out.append(jnp.where(lane < 64, even, odd))
            both = roll(jnp.where(lane < 64, odd, even), 16 * k)
            tail = both if tail is None else jnp.where((lane & 63) >= 16 * k, both, tail)
        out.append(tail)
    return out


def build_taps(w, t_ref):
    for dx in range(5):
        pieces = [w(dy, dx).astype(F32) for dy in range(5)]
        base = jnp.concatenate(pieces + [jnp.zeros((CH, KROWS - 5 * CH), F32)], axis=1)
        for y in range(ROWS):
            t_ref[CH * y : CH * (y + 1), KROWS * dx : KROWS * (dx + 1)] = roll(base, CH * y).astype(BF16)


def bias_column(bias_row, channel_major):
    shape = (BLK, CH)
    i = row_ids(shape)
    owner = (i >> 3) if channel_major else (i & 31)
    spread = jnp.where(owner == lane_ids(shape), jnp.broadcast_to(bias_row, shape), 0.0)
    return jnp.broadcast_to(jnp.sum(spread, axis=1, keepdims=True), (BLK, LANES))


def kernel(
    cams,
    ev_hbm, w1_hbm, wm_hbm, b1_hbm, bm_hbm, rows_hbm, wts_hbm,
    vol_ref, feat_ref,
    ev_ref, w1_ref, wm_ref, b1_ref, bm_ref, rows_ref, wts_ref,
    win, wrecv, x1, x2, x3, t1, t2, t3, bias, fblk, frx, fown, fpart, fback, macc, msend, mrecv, mval, featf, wide, tab,
    in_sem, s1_send, s1_recv, f_send, f_recv, o_send, o_recv, m_send, m_recv,
):
    cam = lax.axis_index("cam")
    me = lax.axis_index("row")
    odd = lax.rem(cam, 2)
    far = (lax.rem(cam + cams - 1 + 2 * odd, cams), me)
    near = (cam + 1 - 2 * odd, me)
    peers = [lax.rem(me + k, BANDS) for k in range(1, BANDS)]

    barrier = pltpu.get_barrier_semaphore()
    for peer in peers:
        pl.semaphore_signal(barrier, inc=1, device_id=(cam, peer), device_id_type=MESH)
    for peer in (far, near):
        pl.semaphore_signal(barrier, inc=1, device_id=peer, device_id_type=MESH)
    loads = [
        pltpu.make_async_copy(src, dst, in_sem.at[n])
        for n, (src, dst) in enumerate(
            (
                (ev_hbm, ev_ref), (w1_hbm, w1_ref), (wm_hbm, wm_ref), (b1_hbm, b1_ref),
                (bm_hbm, bm_ref), (rows_hbm, rows_ref), (wts_hbm, wts_ref),
            )
        )
    ]
    for load in loads:
        load.start()
    loads[0].wait()

    ev = jnp.dot(row_major_perm(), ev_ref[...], preferred_element_type=F32)
    tiles = [ev[:, LANES * t : LANES * (t + 1)].astype(BF16) for t in range(TILES)]
    for strip in range(BANDS):
        win[strip] = pack_window(window_of(tiles, strip))

    pl.semaphore_wait(barrier, BANDS + 1)

    def s1_copy(dst, src_row):
        return pltpu.make_async_remote_copy(
            src_ref=win.at[dst],
            dst_ref=wrecv.at[src_row],
            send_sem=s1_send.at[dst],
            recv_sem=s1_recv.at[src_row],
            device_id=(cam, dst),
            device_id_type=MESH,
        )

    for peer in peers:
        s1_copy(peer, me).start()
    wrecv[me] = win[me]

    for load in loads[1:]:
        load.wait()

    zero_edge = jnp.zeros((EDGE, LANES), BF16)
    for x in (x1, x2, x3):
        for dx in range(5):
            x[dx, 0:EDGE] = zero_edge
            x[dx, EDGE + BANDS * BLK :] = zero_edge
    build_taps(lambda dy, dx: w1_ref[dy, dx], t1)
    build_taps(lambda dy, dx: wm_ref[0, dy, dx], t2)
    build_taps(lambda dy, dx: wm_ref[1, dy, dx], t3)
    perm = channel_major_perm()
    for dx in range(5):
        cols = slice(KROWS * dx, KROWS * (dx + 1))
        t3[:, cols] = jnp.dot(perm, t3[:, cols], preferred_element_type=F32).astype(BF16)
    bias[0] = bias_column(b1_ref[...], False)
    bias[1] = bias_column(bm_ref[0:1], False)
    bias[2] = bias_column(bm_ref[1:2], True)
    for d in range(2):
        edge = jnp.zeros((GROUPS * PACK, ROWS, LANES), F32)
        fpart[d, :, 0:ROWS] = edge
        fpart[d, :, ROWS * (BANDS + 1) :] = edge

    first = me * ROWS
    shape = (ROWS, LANES)
    pick = (
        ((row_ids((PLANES * ROWS, 4 * LANES)) & 7) * 64 + (row_ids((PLANES * ROWS, 4 * LANES)) >> 3))
        == lane_ids((PLANES * ROWS, 4 * LANES))
    ).astype(BF16)
    serving = first + row_ids((ROWS, PLANES)) - REACH
    parts = []
    for kind in range(2):
        d = odd if kind == 0 else 1 - odd
        for o in range(SPAN):
            total = jnp.zeros((ROWS, PLANES), F32)
            for k in range(4):
                hit = rows_ref[d, :, k] == serving + o
                total = total + jnp.where(hit, wts_ref[d, :, k], 0.0)
            total = total * (1.0 / CH)
            doubled = jnp.concatenate([total, jnp.zeros((ROWS, 64 - PLANES), F32)], axis=1)
            doubled = jnp.concatenate([doubled, doubled], axis=1)
            half = lane_ids(shape) >> 6
            parts.append(
                jnp.concatenate(
                    [jnp.where(row_ids(shape) == 2 * j + half, doubled, 0.0) for j in range(4)], axis=1
                )
            )
    table = jnp.concatenate(parts, axis=0)
    high = table.astype(BF16)
    low = (table - high.astype(F32)).astype(BF16)
    for n, piece in enumerate((high, low)):
        tab[n] = lax.dot_general(
            pick, piece, (((1,), (1,)), ((), ())), preferred_element_type=F32
        ).astype(BF16)

    for k in range(1, BANDS):
        s1_copy(peers[0], lax.rem(me + BANDS - k, BANDS)).wait_recv()

    column = lane_ids((1, LANES)) + me * STRIP - HALO
    inside = jnp.logical_and(column >= 0, column < COLS)

    def put(x, b, value):
        for dx in range(5):
            x[dx, EDGE + BLK * b : EDGE + BLK * (b + 1)] = roll(value, 2 - dx)

    def conv(x, t, pair):
        halves = [
            jnp.concatenate([x[dx, BLK * b : BLK * b + KROWS] for dx in range(5)], axis=0)
            for b in (2 * pair, 2 * pair + 1)
        ]
        return jnp.dot(t[...], jnp.concatenate(halves, axis=1), preferred_element_type=F32)

    def hidden(x, t, number, y, pair):
        out = conv(x, t, pair)
        for h in range(2):
            value = jnp.maximum(out[:, LANES * h : LANES * (h + 1)] + bias[number], 0.0)
            put(y, 2 * pair + h, jnp.where(inside, value, 0.0).astype(BF16))

    def f_copy(kind, b):
        return pltpu.make_async_remote_copy(
            src_ref=fblk.at[b],
            dst_ref=frx.at[kind, b],
            send_sem=f_send.at[kind, b],
            recv_sem=f_recv.at[kind, b],
            device_id=far if kind == 0 else near,
            device_id_type=MESH,
        )

    def o_copy(dst, strip):
        return pltpu.make_async_remote_copy(
            src_ref=fblk.at[dst],
            dst_ref=fback.at[strip],
            send_sem=o_send.at[dst],
            recv_sem=o_recv.at[strip],
            device_id=(cam, dst),
            device_id_type=MESH,
        )

    def last(pair):
        out = conv(x3, t3, pair)
        for h in range(2):
            b = 2 * pair + h
            value = out[:, LANES * h : LANES * (h + 1)] + bias[2]
            packed = jnp.concatenate(pack_features(value.reshape(CH, ROWS, LANES)), axis=0)
            packed = packed.astype(BF16)
            fblk[b] = packed
            fown[:, ROWS * b : ROWS * (b + 1)] = packed.astype(F32).reshape(GROUPS * PACK, ROWS, LANES)
            for kind in range(2):
                f_copy(kind, b).start()

            @pl.when(me != b)
            def _():
                o_copy(b, me).start()

    pairs = BANDS // 2
    for b in range(BANDS):
        put(x1, b, unpack_window(wrecv[b]))
    for step in range(pairs + 2):
        if step < pairs:
            hidden(x1, t1, 0, x2, step)
        if 0 <= step - 1 < pairs:
            hidden(x2, t2, 1, x3, step - 1)
        if 0 <= step - 2 < pairs:
            last(step - 2)

    fback[me] = fblk[me]

    def m_copy(kind, dst, strip):
        return pltpu.make_async_remote_copy(
            src_ref=msend.at[kind, dst],
            dst_ref=mrecv.at[kind, strip],
            send_sem=m_send.at[kind, dst],
            recv_sem=m_recv.at[kind, strip],
            device_id=(cam, dst),
            device_id_type=MESH,
        )

    def arrive(kind, b):
        f_copy(kind, b).wait_recv()
        fpart[kind, :, ROWS * (b + 1) : ROWS * (b + 2)] = (
            frx[kind, b].astype(F32).reshape(GROUPS * PACK, ROWS, LANES)
        )

    def match(kind, b):
        def products(n, acc):
            own = fown[n, ROWS * b : ROWS * (b + 1)]
            return tuple(
                acc[o] + own * fpart[kind, n, ROWS * (b + 1) + o - REACH : ROWS * (b + 2) + o - REACH]
                for o in range(SPAN)
            )

        def group(g, accs):
            main, tail = accs
            for k in range(4):
                main = products(PACK * g + k, main)
            return main, products(PACK * g + 4, tail)

        zeros = tuple(jnp.zeros((ROWS, LANES), F32) for _ in range(SPAN))
        accs = lax.fori_loop(0, GROUPS, group, (zeros, zeros), unroll=True)
        for n in range(2):
            for o in range(SPAN):
                macc[n, o, ROWS * b : ROWS * (b + 1)] = accs[n][o]

    def finish(kind, first):
        count = ROWS * BANDS // 2
        rows = slice(ROWS * first, ROWS * first + count)
        lane = lane_ids((count, LANES))
        main = [macc[0, o, rows] for o in range(SPAN)]
        tail = [macc[1, o, rows] for o in range(SPAN)]
        out = [fold(lane, 64, main[2 * k], main[2 * k + 1]) for k in range(4)]
        ends = [fold(lane, 64, tail[o], tail[o + 4]) for o in range(4)]
        ends = [fold(lane, 32, ends[o], ends[o + 2]) for o in range(2)]
        out.append(fold(lane, 16, ends[0], ends[1]))
        last_tail = tail[8]
        for step in (64, 32, 16):
            last_tail = last_tail + roll(last_tail, step)
        out.append(jnp.where(lane < 64, main[8] + roll(main[8], 64), last_tail))
        for n in range(BANDS // 2):
            part = [v[ROWS * n : ROWS * (n + 1)] for v in out]
            msend[kind, first + n] = jnp.concatenate(part, axis=0).astype(BF16)

    for kind in (1, 0):
        arrive(kind, 0)
        for b in range(BANDS):
            if b + 1 < BANDS:
                arrive(kind, b + 1)
            match(kind, b)
        for first in (0, BANDS // 2):
            finish(kind, first)
        for peer in peers:
            m_copy(kind, peer, me).start()
        mrecv[kind, me] = msend[kind, me]

    for k in range(1, BANDS):
        o_copy(peers[0], lax.rem(me + BANDS - k, BANDS)).wait_recv()
    for c in range(CH):
        g, k, h = c >> 3, (c & 7) >> 1, c & 1
        body = (PACK * g + k) * ROWS
        ends = (PACK * g + 4) * ROWS
        end_lane = 16 * k if h else 64 + 16 * k
        pieces = []
        for s in range(BANDS):
            pieces.append((lambda s=s: wide[s, body : body + ROWS], 64 * h, STRIP * s, 64))
            pieces.append((lambda s=s: wide[s, ends : ends + ROWS], end_lane, STRIP * s + 64, 16))
        if c == 0:
            for s in range(BANDS):
                wide[s] = fback[s].astype(F32)
        for t in range(TILES):
            featf[ROWS * c : ROWS * (c + 1), LANES * t : LANES * (t + 1)] = place(pieces, t)
    feat_ref[...] = featf[...].astype(BF16)

    for kind in (1, 0):
        for k in range(1, BANDS):
            m_copy(kind, peers[0], lax.rem(me + BANDS - k, BANDS)).wait_recv()
        for s in range(BANDS):
            wide[s, 0:MPACK] = mrecv[kind, s].astype(F32)
        for o in range(SPAN):
            body = 8 * (o >> 1) if o < 8 else 5 * ROWS
            body_lane = 64 * (o & 1) if o < 8 else 0
            ends = 4 * ROWS if o < 8 else 5 * ROWS
            end_lane = 16 * o if o < 8 else 64
            pieces = []
            for s in range(BANDS):
                pieces.append((lambda s=s: wide[s, body : body + ROWS], body_lane, STRIP * s, 64))
                pieces.append((lambda s=s: wide[s, ends : ends + ROWS], end_lane, STRIP * s + 64, 16))
            start = MROWS * kind + ROWS * o
            for t in range(TILES):
                mval[start : start + ROWS, LANES * t : LANES * (t + 1)] = place(pieces, t)
    values = mval[...].astype(BF16)
    out = jnp.dot(tab[0], values, preferred_element_type=F32)
    out = out + jnp.dot(tab[1], values, preferred_element_type=F32)
    vol_ref[...] = out.astype(BF16)

    for peer in peers:
        s1_copy(peer, me).wait_send()
        o_copy(peer, me).wait_send()
        for kind in range(2):
            m_copy(kind, peer, me).wait_send()
    for b in range(BANDS):
        for kind in range(2):
            f_copy(kind, b).wait_send()


def local(cams, events, conv_in, bias_in, conv_mid, bias_mid, tap_rows, tap_weights):
    dma = pltpu.SemaphoreType.DMA
    vmem = pl.BlockSpec(memory_space=pltpu.VMEM)
    padded = (5, BANDS * BLK + 2 * EDGE, LANES)
    taps = (BLK, 5 * KROWS)
    operands = (
        events.reshape(BLK, COLS),
        conv_in.transpose(2, 3, 0, 1),
        conv_mid.transpose(0, 3, 4, 1, 2),
        bias_in.reshape(1, CH),
        bias_mid,
        tap_rows.transpose(0, 2, 3, 1),
        tap_weights.transpose(0, 2, 3, 1),
    )
    vol, feat = pl.pallas_call(
        functools.partial(kernel, cams),
        out_shape=(
            pltpu.VMEM((PLANES * ROWS, COLS), BF16),
            pltpu.VMEM((BLK, COLS), BF16),
        ),
        in_specs=[pl.BlockSpec(memory_space=pltpu.HBM)] * 7,
        out_specs=(vmem, vmem),
        scratch_shapes=[
            *[pltpu.VMEM(operand.shape, operand.dtype) for operand in operands],
            pltpu.VMEM((BANDS, WROWS, LANES), BF16),
            pltpu.VMEM((BANDS, WROWS, LANES), BF16),
            pltpu.VMEM(padded, BF16),
            pltpu.VMEM(padded, BF16),
            pltpu.VMEM(padded, BF16),
            pltpu.VMEM(taps, BF16),
            pltpu.VMEM(taps, BF16),
            pltpu.VMEM(taps, BF16),
            pltpu.VMEM((3, BLK, LANES), F32),
            pltpu.VMEM((BANDS, FROWS, LANES), BF16),
            pltpu.VMEM((2, BANDS, FROWS, LANES), BF16),
            pltpu.VMEM((GROUPS * PACK, ROWS * BANDS, LANES), F32),
            pltpu.VMEM((2, GROUPS * PACK, ROWS * (BANDS + 2), LANES), F32),
            pltpu.VMEM((BANDS, FROWS, LANES), BF16),
            pltpu.VMEM((2, SPAN, ROWS * BANDS, LANES), F32),
            pltpu.VMEM((2, BANDS, MPACK, LANES), BF16),
            pltpu.VMEM((2, BANDS, MPACK, LANES), BF16),
            pltpu.VMEM((2 * MROWS, COLS), F32),
            pltpu.VMEM((BLK, COLS), F32),
            pltpu.VMEM((BANDS, FROWS, LANES), F32),
            pltpu.VMEM((2, PLANES * ROWS, 2 * MROWS), BF16),
            dma((7,)),
            dma((BANDS,)), dma((BANDS,)),
            dma((2, BANDS)), dma((2, BANDS)),
            dma((BANDS,)), dma((BANDS,)),
            dma((2, BANDS)), dma((2, BANDS)),
        ],
        compiler_params=pltpu.CompilerParams(
            collective_id=0, has_side_effects=True, vmem_limit_bytes=48 * 1024 * 1024
        ),
    )(*[pltpu.with_memory_space_constraint(operand, pltpu.HBM) for operand in operands])
    return vol.reshape(1, PLANES, ROWS, COLS), feat.reshape(1, CH, ROWS, COLS)


def solution(mesh):
    in_specs = (
        P("cam", None, "row", None),
        P(),
        P(),
        P(),
        P(),
        P(None, None, "row", None),
        P(None, None, "row", None),
    )
    out_specs = (P("cam", None, "row", None), P("cam", None, "row", None))
    return jax.shard_map(
        functools.partial(local, mesh.shape["cam"]),
        mesh=mesh,
        in_specs=in_specs,
        out_specs=out_specs,
        check_vma=False,
    )
```

```python
import functools

import jax
import jax.numpy as jnp
from jax import lax
from jax.experimental import pallas as pl
from jax.experimental.pallas import tpu as pltpu
from jax.sharding import PartitionSpec as P

MESH = pl.DeviceIdType.MESH
F32 = jnp.float32
BF16 = jnp.bfloat16

CH = 32
BANDS = 8
ROWS = 8
COLS = 640
STRIP = COLS // BANDS
HALO = 6
LANES = 128
TILES = COLS // LANES
BLK = CH * ROWS
EDGE = 2 * CH
KROWS = BLK + 2 * EDGE
PLANES = 48
SPAN = 9
REACH = 4
MROWS = SPAN * ROWS
GROUPS = 4
PACK = 5
FROWS = GROUPS * PACK * ROWS
MPACK = 6 * ROWS
QUARTER = BLK // 4
WROWS = 3 * QUARTER


def lane_ids(shape):
    return lax.broadcasted_iota(jnp.int32, shape, 1)


def row_ids(shape):
    return lax.broadcasted_iota(jnp.int32, shape, 0)


def roll(value, shift):
    shift = shift % value.shape[1]
    return value if shift == 0 else pltpu.roll(value, shift, 1)


def row_major_perm():
    shape = (BLK, BLK)
    i, j = row_ids(shape), lane_ids(shape)
    return ((i & 31) * ROWS + (i >> 5) == j).astype(BF16)


def channel_major_perm():
    shape = (BLK, BLK)
    i, j = row_ids(shape), lane_ids(shape)
    return ((i & 7) * CH + (i >> 3) == j).astype(BF16)


def window_of(tiles, strip):
    start = STRIP * strip - HALO
    first = start // LANES
    off = start - first * LANES
    shape = tiles[0].shape
    low = roll(tiles[first], -off) if first >= 0 else jnp.zeros(shape, BF16)
    if LANES - off >= STRIP + 2 * HALO:
        return low
    high = roll(tiles[first + 1], -off) if first + 1 < TILES else jnp.zeros(shape, BF16)
    return jnp.where(lane_ids(shape) < LANES - off, low, high)


def pack_window(value):
    lane = lane_ids((QUARTER, LANES))
    parts = [value[QUARTER * g : QUARTER * (g + 1)] for g in range(4)]
    pairs = [jnp.where(lane < 64, parts[g], roll(parts[g + 1], 64)) for g in (0, 2)]
    tail = roll(parts[0], -64)
    for g in range(1, 4):
        tail = jnp.where(lane >= 32 * g, roll(parts[g], 32 * g - 64), tail)
    return jnp.concatenate(pairs + [tail], axis=0)


def unpack_window(packed):
    lane = lane_ids((QUARTER, LANES))
    tail = packed[2 * QUARTER :]
    parts = []
    for g in range(4):
        pair = packed[QUARTER * (g // 2) : QUARTER * (g // 2 + 1)]
        parts.append(jnp.where(lane < 64, roll(pair, 64 * (g & 1)), roll(tail, 64 - 32 * g)))
    return jnp.concatenate(parts, axis=0)


def fold(lane, step, even, odd):
    clear = (lane & step) == 0
    own = jnp.where(clear, even, odd)
    other = jnp.where(clear, odd, even)
    if step == 64:
        return own + roll(other, 64)
    return own + jnp.where(clear, roll(other, -step), roll(other, step))


def place(pieces, tile):
    out = None
    for get, lane, column, count in pieces:
        lo = max(column, LANES * tile) - LANES * tile
        hi = min(column + count, LANES * (tile + 1)) - LANES * tile
        if lo < hi:
            value = roll(get(), column - LANES * tile - lane)
            out = value if out is None else jnp.where(lane_ids(value.shape) >= lo, value, out)
    return out


def pack_features(value):
    lane = lane_ids((ROWS, LANES))
    out = []
    for g in range(GROUPS):
        tail = None
        for k in range(4):
            even = roll(value[8 * g + 2 * k], -HALO)
            odd = roll(value[8 * g + 2 * k + 1], 64 - HALO)
            out.append(jnp.where(lane < 64, even, odd))
            both = roll(jnp.where(lane < 64, odd, even), 16 * k)
            tail = both if tail is None else jnp.where((lane & 63) >= 16 * k, both, tail)
        out.append(tail)
    return out


def build_taps(w, t_ref):
    for dx in range(5):
        pieces = [w(dy, dx).astype(F32) for dy in range(5)]
        base = jnp.concatenate(pieces + [jnp.zeros((CH, KROWS - 5 * CH), F32)], axis=1)
        for y in range(ROWS):
            t_ref[CH * y : CH * (y + 1), KROWS * dx : KROWS * (dx + 1)] = roll(base, CH * y).astype(BF16)


def bias_column(bias_row, channel_major):
    shape = (BLK, CH)
    i = row_ids(shape)
    owner = (i >> 3) if channel_major else (i & 31)
    spread = jnp.where(owner == lane_ids(shape), jnp.broadcast_to(bias_row, shape), 0.0)
    return jnp.broadcast_to(jnp.sum(spread, axis=1, keepdims=True), (BLK, LANES))


def kernel(
    cams,
    ev_hbm, w1_hbm, wm_hbm, b1_hbm, bm_hbm, rows_hbm, wts_hbm,
    vol_ref, feat_ref,
    ev_ref, w1_ref, wm_ref, b1_ref, bm_ref, rows_ref, wts_ref,
    win, wrecv, x1, x2, x3, t1, t2, t3, bias, fblk, frx, fown, fpart, fback, macc, msend, mrecv, mval, volf, featf, wide, tab,
    in_sem, s1_send, s1_recv, f_send, f_recv, o_send, o_recv, m_send, m_recv, seam_send, far_sem,
):
    cam = lax.axis_index("cam")
    me = lax.axis_index("row")
    odd = lax.rem(cam, 2)
    far = (lax.rem(cam + cams - 1 + 2 * odd, cams), me)
    near = (cam + 1 - 2 * odd, me)
    peers = [lax.rem(me + k, BANDS) for k in range(1, BANDS)]

    barrier = pltpu.get_barrier_semaphore()
    for peer in peers:
        pl.semaphore_signal(barrier, inc=1, device_id=(cam, peer), device_id_type=MESH)
    pl.semaphore_signal(barrier, inc=1, device_id=near, device_id_type=MESH)

    place_in_run = lax.rem(cam, cams // 2)
    late = place_in_run == cams // 2 - 1
    early = place_in_run == 0

    @pl.when(jnp.logical_not(late))
    def _():
        pl.semaphore_signal(barrier, inc=1, device_id=far, device_id_type=MESH)

    @pl.when(early)
    def _():
        for peer in peers:
            pl.semaphore_signal(barrier, inc=1, device_id=(far[0], peer), device_id_type=MESH)

    loads = [
        pltpu.make_async_copy(src, dst, in_sem.at[n])
        for n, (src, dst) in enumerate(
            (
                (ev_hbm, ev_ref), (w1_hbm, w1_ref), (wm_hbm, wm_ref), (b1_hbm, b1_ref),
                (bm_hbm, bm_ref), (rows_hbm, rows_ref), (wts_hbm, wts_ref),
            )
        )
    ]
    for load in loads:
        load.start()
    loads[0].wait()

    ev = jnp.dot(row_major_perm(), ev_ref[...], preferred_element_type=F32)
    tiles = [ev[:, LANES * t : LANES * (t + 1)].astype(BF16) for t in range(TILES)]
    for strip in range(BANDS):
        win[strip] = pack_window(window_of(tiles, strip))

    expected = BANDS + 1 + (BANDS - 1) * late.astype(jnp.int32) - early.astype(jnp.int32)
    pl.semaphore_wait(barrier, expected)

    def s1_copy(dst, src_row):
        return pltpu.make_async_remote_copy(
            src_ref=win.at[dst],
            dst_ref=wrecv.at[src_row],
            send_sem=s1_send.at[dst],
            recv_sem=s1_recv.at[src_row],
            device_id=(cam, dst),
            device_id_type=MESH,
        )

    for peer in peers:
        s1_copy(peer, me).start()
    wrecv[me] = win[me]

    @pl.when(late)
    def _():
        pl.semaphore_signal(far_sem, inc=1, device_id=far, device_id_type=MESH)


    for load in loads[1:]:
        load.wait()

    zero_edge = jnp.zeros((EDGE, LANES), BF16)
    for x in (x1, x2, x3):
        for dx in range(5):
            x[dx, 0:EDGE] = zero_edge
            x[dx, EDGE + BANDS * BLK :] = zero_edge
    build_taps(lambda dy, dx: w1_ref[dy, dx], t1)
    build_taps(lambda dy, dx: wm_ref[0, dy, dx], t2)
    build_taps(lambda dy, dx: wm_ref[1, dy, dx], t3)
    perm = channel_major_perm()
    for dx in range(5):
        cols = slice(KROWS * dx, KROWS * (dx + 1))
        t3[:, cols] = jnp.dot(perm, t3[:, cols], preferred_element_type=F32).astype(BF16)
    bias[0] = bias_column(b1_ref[...], False)
    bias[1] = bias_column(bm_ref[0:1], False)
    bias[2] = bias_column(bm_ref[1:2], True)
    for d in range(2):
        edge = jnp.zeros((GROUPS * PACK, ROWS, LANES), F32)
        fpart[d, :, 0:ROWS] = edge
        fpart[d, :, ROWS * (BANDS + 1) :] = edge
    fown[:, 0:ROWS] = edge
    fown[:, ROWS * (BANDS + 1) :] = edge

    first = me * ROWS
    shape = (ROWS, LANES)
    pick = (
        ((row_ids((PLANES * ROWS, 4 * LANES)) & 7) * 64 + (row_ids((PLANES * ROWS, 4 * LANES)) >> 3))
        == lane_ids((PLANES * ROWS, 4 * LANES))
    ).astype(BF16)
    serving = first + row_ids((ROWS, PLANES)) - REACH
    for kind in range(2):
        parts = []
        d = odd if kind == 0 else 1 - odd
        for o in range(SPAN):
            total = jnp.zeros((ROWS, PLANES), F32)
            for k in range(4):
                hit = rows_ref[d, :, k] == serving + o
                total = total + jnp.where(hit, wts_ref[d, :, k], 0.0)
            total = total * (1.0 / CH)
            doubled = jnp.concatenate([total, jnp.zeros((ROWS, 64 - PLANES), F32)], axis=1)
            doubled = jnp.concatenate([doubled, doubled], axis=1)
            half = lane_ids(shape) >> 6
            parts.append(
                jnp.concatenate(
                    [jnp.where(row_ids(shape) == 2 * j + half, doubled, 0.0) for j in range(4)], axis=1
                )
            )
        table = jnp.concatenate(parts, axis=0)
        high = table.astype(BF16).astype(F32)
        table = jnp.concatenate([high, table - high], axis=0).astype(BF16)
        tab[kind] = lax.dot_general(
            pick, table, (((1,), (1,)), ((), ())), preferred_element_type=F32
        ).astype(BF16)

    for k in range(1, BANDS):
        s1_copy(peers[0], lax.rem(me + BANDS - k, BANDS)).wait_recv()

    column = lane_ids((1, LANES)) + me * STRIP - HALO
    inside = jnp.logical_and(column >= 0, column < COLS)

    def put(x, b, value):
        for dx in range(5):
            x[dx, EDGE + BLK * b : EDGE + BLK * (b + 1)] = roll(value, 2 - dx)

    def conv(x, t, pair):
        halves = [
            jnp.concatenate([x[dx, BLK * b : BLK * b + KROWS] for dx in range(5)], axis=0)
            for b in (2 * pair, 2 * pair + 1)
        ]
        return jnp.dot(t[...], jnp.concatenate(halves, axis=1), preferred_element_type=F32)

    def hidden(x, t, number, y, pair):
        out = conv(x, t, pair)
        for h in range(2):
            value = jnp.maximum(out[:, LANES * h : LANES * (h + 1)] + bias[number], 0.0)
            put(y, 2 * pair + h, jnp.where(inside, value, 0.0).astype(BF16))

    def f_copy(kind, b):
        return pltpu.make_async_remote_copy(
            src_ref=fblk.at[b],
            dst_ref=frx.at[kind, b],
            send_sem=f_send.at[kind, b],
            recv_sem=f_recv.at[kind, b],
            device_id=far if kind == 0 else near,
            device_id_type=MESH,
        )

    def o_copy(dst, strip):
        return pltpu.make_async_remote_copy(
            src_ref=fblk.at[dst],
            dst_ref=fback.at[strip],
            send_sem=o_send.at[dst],
            recv_sem=o_recv.at[strip],
            device_id=(cam, dst),
            device_id_type=MESH,
        )

    def last(pair):
        out = conv(x3, t3, pair)
        for h in range(2):
            b = 2 * pair + h
            value = out[:, LANES * h : LANES * (h + 1)] + bias[2]
            packed = jnp.concatenate(pack_features(value.reshape(CH, ROWS, LANES)), axis=0)
            packed = packed.astype(BF16)
            fblk[b] = packed
            fown[:, ROWS * (b + 1) : ROWS * (b + 2)] = packed.astype(F32).reshape(
                GROUPS * PACK, ROWS, LANES
            )

        @pl.when(jnp.logical_not(late))
        def _():
            for h in range(2):
                f_copy(0, 2 * pair + h).start()

        for h in range(2):
            f_copy(1, 2 * pair + h).start()
        for h in range(2):

            @pl.when(me != 2 * pair + h)
            def _(b=2 * pair + h):
                o_copy(b, me).start()

    pairs = BANDS // 2
    for b in range(BANDS):
        put(x1, b, unpack_window(wrecv[b]))
    for step in range(pairs + 2):
        if step < pairs:
            hidden(x1, t1, 0, x2, step)
        if 0 <= step - 1 < pairs:
            hidden(x2, t2, 1, x3, step - 1)
        if step == 2:

            @pl.when(early)
            def _():
                pl.semaphore_wait(far_sem, 1)

        if 0 <= step - 2 < pairs:
            last(step - 2)

    fback[me] = fblk[me]

    def m_copy(kind, dst, strip):
        return pltpu.make_async_remote_copy(
            src_ref=msend.at[kind, dst],
            dst_ref=mrecv.at[kind, strip],
            send_sem=m_send.at[kind, dst],
            recv_sem=m_recv.at[kind, strip],
            device_id=(cam, dst),
            device_id_type=MESH,
        )

    def arrive(kind, b):
        f_copy(kind, b).wait_recv()
        fpart[kind, :, ROWS * (b + 1) : ROWS * (b + 2)] = (
            frx[kind, b].astype(F32).reshape(GROUPS * PACK, ROWS, LANES)
        )

    def match(own_ref, part_ref, b):
        def products(n, acc):
            own = own_ref[n, ROWS * (b + 1) : ROWS * (b + 2)]
            return tuple(
                acc[o] + own * part_ref[n, ROWS * (b + 1) + o - REACH : ROWS * (b + 2) + o - REACH]
                for o in range(SPAN)
            )

        def group(g, accs):
            main, tail = accs
            for k in range(4):
                main = products(PACK * g + k, main)
            return main, products(PACK * g + 4, tail)

        zeros = tuple(jnp.zeros((ROWS, LANES), F32) for _ in range(SPAN))
        accs = lax.fori_loop(0, GROUPS, group, (zeros, zeros), unroll=True)
        for n in range(2):
            for o in range(SPAN):
                macc[n, o, ROWS * b : ROWS * (b + 1)] = accs[n][o]

    def finish(kind, first):
        count = ROWS * BANDS // 2
        rows = slice(ROWS * first, ROWS * first + count)
        lane = lane_ids((count, LANES))
        main = [macc[0, o, rows] for o in range(SPAN)]
        tail = [macc[1, o, rows] for o in range(SPAN)]
        out = [fold(lane, 64, main[2 * k], main[2 * k + 1]) for k in range(4)]
        ends = [fold(lane, 64, tail[o], tail[o + 4]) for o in range(4)]
        ends = [fold(lane, 32, ends[o], ends[o + 2]) for o in range(2)]
        out.append(fold(lane, 16, ends[0], ends[1]))
        last_tail = tail[8]
        for step in (64, 32, 16):
            last_tail = last_tail + roll(last_tail, step)
        out.append(jnp.where(lane < 64, main[8] + roll(main[8], 64), last_tail))
        for n in range(BANDS // 2):
            part = [v[ROWS * n : ROWS * (n + 1)] for v in out]
            msend[kind, first + n] = jnp.concatenate(part, axis=0).astype(BF16)

    def seam_copy(dst):
        return pltpu.make_async_remote_copy(
            src_ref=msend.at[2, dst],
            dst_ref=mrecv.at[0, me],
            send_sem=seam_send.at[dst],
            recv_sem=m_recv.at[0, me],
            device_id=(far[0], dst),
            device_id_type=MESH,
        )

    @pl.when(late)
    def _():
        for b in range(BANDS):
            arrive(0, b)
        for b in range(BANDS):
            match(fpart.at[0], fown, b)
        for first_block in (0, BANDS // 2):
            finish(2, first_block)
        for dst in range(BANDS):
            seam_copy(dst).start()

    arrive(1, 0)
    for b in range(BANDS):
        if b + 1 < BANDS:
            arrive(1, b + 1)
        match(fown, fpart.at[1], b)
    for first_block in (0, BANDS // 2):
        finish(1, first_block)
    for peer in peers:
        m_copy(1, peer, me).start()
    mrecv[1, me] = msend[1, me]

    @pl.when(jnp.logical_not(early))
    def _():
        @pl.when(jnp.logical_not(late))
        def _():
            for b in range(BANDS):
                arrive(0, b)

        for b in range(BANDS):
            match(fown, fpart.at[0], b)
        for first_block in (0, BANDS // 2):
            finish(0, first_block)
        for peer in peers:
            m_copy(0, peer, me).start()
        mrecv[0, me] = msend[0, me]

    for k in range(1, BANDS):
        o_copy(peers[0], lax.rem(me + BANDS - k, BANDS)).wait_recv()
    for c in range(CH):
        g, k, h = c >> 3, (c & 7) >> 1, c & 1
        body = (PACK * g + k) * ROWS
        ends = (PACK * g + 4) * ROWS
        end_lane = 16 * k if h else 64 + 16 * k
        pieces = []
        for s in range(BANDS):
            pieces.append((lambda s=s: wide[s, body : body + ROWS], 64 * h, STRIP * s, 64))
            pieces.append((lambda s=s: wide[s, ends : ends + ROWS], end_lane, STRIP * s + 64, 16))
        if c == 0:
            for s in range(BANDS):
                wide[s] = fback[s].astype(F32)
        for t in range(TILES):
            featf[ROWS * c : ROWS * (c + 1), LANES * t : LANES * (t + 1)] = place(pieces, t)
    feat_ref[...] = featf[...].astype(BF16)

    for kind in (1, 0):
        if kind == 0:

            @pl.when(early)
            def _():
                m_copy(0, peers[0], me).wait_recv()

        for k in range(1, BANDS):
            m_copy(kind, peers[0], lax.rem(me + BANDS - k, BANDS)).wait_recv()
        for s in range(BANDS):
            wide[s, 0:MPACK] = mrecv[kind, s].astype(F32)
        for o in range(SPAN):
            body = 8 * (o >> 1) if o < 8 else 5 * ROWS
            body_lane = 64 * (o & 1) if o < 8 else 0
            ends = 4 * ROWS if o < 8 else 5 * ROWS
            end_lane = 16 * o if o < 8 else 64
            pieces = []
            for s in range(BANDS):
                pieces.append((lambda s=s: wide[s, body : body + ROWS], body_lane, STRIP * s, 64))
                pieces.append((lambda s=s: wide[s, ends : ends + ROWS], end_lane, STRIP * s + 64, 16))
            start = ROWS * o
            for t in range(TILES):
                mval[start : start + ROWS, LANES * t : LANES * (t + 1)] = place(pieces, t)
        values = mval[...]
        values = jnp.concatenate([values, values], axis=0).astype(BF16)
        out = jnp.dot(tab[kind], values, preferred_element_type=F32)
        if kind == 1:
            volf[...] = out
        else:
            vol_ref[...] = (volf[...] + out).astype(BF16)

    for peer in peers:
        s1_copy(peer, me).wait_send()
        o_copy(peer, me).wait_send()
        m_copy(1, peer, me).wait_send()
    for b in range(BANDS):
        f_copy(1, b).wait_send()

    @pl.when(jnp.logical_not(early))
    def _():
        for peer in peers:
            m_copy(0, peer, me).wait_send()

    @pl.when(late)
    def _():
        for dst in range(BANDS):
            seam_copy(dst).wait_send()

    @pl.when(jnp.logical_not(late))
    def _():
        for b in range(BANDS):
            f_copy(0, b).wait_send()


def store(vol, feat, vol_out, feat_out, sem):
    copies = [
        pltpu.make_async_copy(vol, vol_out, sem.at[0]),
        pltpu.make_async_copy(feat, feat_out, sem.at[1]),
    ]
    for copy in copies:
        copy.start()
    for copy in copies:
        copy.wait()


def local(cams, events, conv_in, bias_in, conv_mid, bias_mid, tap_rows, tap_weights):
    dma = pltpu.SemaphoreType.DMA
    vmem = pl.BlockSpec(memory_space=pltpu.VMEM)
    padded = (5, BANDS * BLK + 2 * EDGE, LANES)
    taps = (BLK, 5 * KROWS)
    operands = (
        events.reshape(BLK, COLS),
        conv_in.transpose(2, 3, 0, 1),
        conv_mid.transpose(0, 3, 4, 1, 2),
        bias_in.reshape(1, CH),
        bias_mid,
        tap_rows.transpose(0, 2, 3, 1),
        tap_weights.transpose(0, 2, 3, 1),
    )
    vol, feat = pl.pallas_call(
        functools.partial(kernel, cams),
        out_shape=(
            pltpu.VMEM((PLANES * ROWS, COLS), BF16),
            pltpu.VMEM((BLK, COLS), BF16),
        ),
        in_specs=[pl.BlockSpec(memory_space=pltpu.HBM)] * 7,
        out_specs=(vmem, vmem),
        scratch_shapes=[
            *[pltpu.VMEM(operand.shape, operand.dtype) for operand in operands],
            pltpu.VMEM((BANDS, WROWS, LANES), BF16),
            pltpu.VMEM((BANDS, WROWS, LANES), BF16),
            pltpu.VMEM(padded, BF16),
            pltpu.VMEM(padded, BF16),
            pltpu.VMEM(padded, BF16),
            pltpu.VMEM(taps, BF16),
            pltpu.VMEM(taps, BF16),
            pltpu.VMEM(taps, BF16),
            pltpu.VMEM((3, BLK, LANES), F32),
            pltpu.VMEM((BANDS, FROWS, LANES), BF16),
            pltpu.VMEM((2, BANDS, FROWS, LANES), BF16),
            pltpu.VMEM((GROUPS * PACK, ROWS * (BANDS + 2), LANES), F32),
            pltpu.VMEM((2, GROUPS * PACK, ROWS * (BANDS + 2), LANES), F32),
            pltpu.VMEM((BANDS, FROWS, LANES), BF16),
            pltpu.VMEM((2, SPAN, ROWS * BANDS, LANES), F32),
            pltpu.VMEM((3, BANDS, MPACK, LANES), BF16),
            pltpu.VMEM((2, BANDS, MPACK, LANES), BF16),
            pltpu.VMEM((MROWS, COLS), F32),
            pltpu.VMEM((PLANES * ROWS, COLS), F32),
            pltpu.VMEM((BLK, COLS), F32),
            pltpu.VMEM((BANDS, FROWS, LANES), F32),
            pltpu.VMEM((2, PLANES * ROWS, 2 * MROWS), BF16),
            dma((7,)),
            dma((BANDS,)), dma((BANDS,)),
            dma((2, BANDS)), dma((2, BANDS)),
            dma((BANDS,)), dma((BANDS,)),
            dma((2, BANDS)), dma((2, BANDS)),
            dma((BANDS,)), pltpu.SemaphoreType.REGULAR,
        ],
        compiler_params=pltpu.CompilerParams(
            collective_id=0, has_side_effects=True, vmem_limit_bytes=48 * 1024 * 1024
        ),
    )(*[pltpu.with_memory_space_constraint(operand, pltpu.HBM) for operand in operands])
    hbm = pl.BlockSpec(memory_space=pltpu.HBM)
    vol, feat = pl.pallas_call(
        store,
        out_shape=(pltpu.HBM(vol.shape, BF16), pltpu.HBM(feat.shape, BF16)),
        in_specs=[vmem, vmem],
        out_specs=(hbm, hbm),
        scratch_shapes=[dma((2,))],
    )(*[pltpu.with_memory_space_constraint(value, pltpu.VMEM) for value in (vol, feat)])
    return vol.reshape(1, PLANES, ROWS, COLS), feat.reshape(1, CH, ROWS, COLS)


def solution(mesh):
    in_specs = (
        P("cam", None, "row", None),
        P(),
        P(),
        P(),
        P(),
        P(None, None, "row", None),
        P(None, None, "row", None),
    )
    out_specs = (P("cam", None, "row", None), P("cam", None, "row", None))
    return jax.shard_map(
        functools.partial(local, mesh.shape["cam"]),
        mesh=mesh,
        in_specs=in_specs,
        out_specs=out_specs,
        check_vma=False,
    )
```

```python
import functools

import jax
import jax.numpy as jnp
from jax import lax
from jax.experimental import pallas as pl
from jax.experimental.pallas import tpu as pltpu
from jax.sharding import PartitionSpec as P

MESH = pl.DeviceIdType.MESH
F32 = jnp.float32
BF16 = jnp.bfloat16

CH = 32
BANDS = 8
ROWS = 8
COLS = 640
STRIP = COLS // BANDS
HALO = 6
LANES = 128
TILES = COLS // LANES
BLK = CH * ROWS
EDGE = 2 * CH
KROWS = BLK + 2 * EDGE
PLANES = 48
SPAN = 9
REACH = 4
MROWS = SPAN * ROWS
GROUPS = 4
PACK = 5
FROWS = GROUPS * PACK * ROWS
MPACK = 6 * ROWS
QUARTER = BLK // 4
WROWS = 3 * QUARTER


def lane_ids(shape):
    return lax.broadcasted_iota(jnp.int32, shape, 1)


def row_ids(shape):
    return lax.broadcasted_iota(jnp.int32, shape, 0)


def roll(value, shift):
    shift = shift % value.shape[1]
    return value if shift == 0 else pltpu.roll(value, shift, 1)


def row_major_perm():
    shape = (BLK, BLK)
    i, j = row_ids(shape), lane_ids(shape)
    return ((i & 31) * ROWS + (i >> 5) == j).astype(BF16)


def channel_major_perm():
    shape = (BLK, BLK)
    i, j = row_ids(shape), lane_ids(shape)
    return ((i & 7) * CH + (i >> 3) == j).astype(BF16)


def window_of(tiles, strip):
    start = STRIP * strip - HALO
    first = start // LANES
    off = start - first * LANES
    shape = tiles[0].shape
    low = roll(tiles[first], -off) if first >= 0 else jnp.zeros(shape, BF16)
    if LANES - off >= STRIP + 2 * HALO:
        return low
    high = roll(tiles[first + 1], -off) if first + 1 < TILES else jnp.zeros(shape, BF16)
    return jnp.where(lane_ids(shape) < LANES - off, low, high)


def pack_window(value):
    lane = lane_ids((QUARTER, LANES))
    parts = [value[QUARTER * g : QUARTER * (g + 1)] for g in range(4)]
    pairs = [jnp.where(lane < 64, parts[g], roll(parts[g + 1], 64)) for g in (0, 2)]
    tail = roll(parts[0], -64)
    for g in range(1, 4):
        tail = jnp.where(lane >= 32 * g, roll(parts[g], 32 * g - 64), tail)
    return jnp.concatenate(pairs + [tail], axis=0)


def unpack_window(packed):
    lane = lane_ids((QUARTER, LANES))
    tail = packed[2 * QUARTER :]
    parts = []
    for g in range(4):
        pair = packed[QUARTER * (g // 2) : QUARTER * (g // 2 + 1)]
        parts.append(jnp.where(lane < 64, roll(pair, 64 * (g & 1)), roll(tail, 64 - 32 * g)))
    return jnp.concatenate(parts, axis=0)


def fold(lane, step, even, odd):
    clear = (lane & step) == 0
    own = jnp.where(clear, even, odd)
    other = jnp.where(clear, odd, even)
    if step == 64:
        return own + roll(other, 64)
    return own + jnp.where(clear, roll(other, -step), roll(other, step))


def place(pieces, tile):
    out = None
    for get, lane, column, count in pieces:
        lo = max(column, LANES * tile) - LANES * tile
        hi = min(column + count, LANES * (tile + 1)) - LANES * tile
        if lo < hi:
            value = roll(get(), column - LANES * tile - lane)
            out = value if out is None else jnp.where(lane_ids(value.shape) >= lo, value, out)
    return out


def pack_features(value):
    lane = lane_ids((ROWS, LANES))
    out = []
    for g in range(GROUPS):
        tail = None
        for k in range(4):
            even = roll(value[8 * g + 2 * k], -HALO)
            odd = roll(value[8 * g + 2 * k + 1], 64 - HALO)
            out.append(jnp.where(lane < 64, even, odd))
            both = roll(jnp.where(lane < 64, odd, even), 16 * k)
            tail = both if tail is None else jnp.where((lane & 63) >= 16 * k, both, tail)
        out.append(tail)
    return out


def build_taps(w, t_ref):
    for dx in range(5):
        pieces = [w(dy, dx).astype(F32) for dy in range(5)]
        base = jnp.concatenate(pieces + [jnp.zeros((CH, KROWS - 5 * CH), F32)], axis=1)
        for y in range(ROWS):
            t_ref[CH * y : CH * (y + 1), KROWS * dx : KROWS * (dx + 1)] = roll(base, CH * y).astype(BF16)


def bias_column(bias_row, channel_major):
    shape = (BLK, CH)
    i = row_ids(shape)
    owner = (i >> 3) if channel_major else (i & 31)
    spread = jnp.where(owner == lane_ids(shape), jnp.broadcast_to(bias_row, shape), 0.0)
    return jnp.broadcast_to(jnp.sum(spread, axis=1, keepdims=True), (BLK, LANES))


def kernel(
    cams,
    ev_hbm, w1_hbm, wm_hbm, b1_hbm, bm_hbm, rows_hbm, wts_hbm,
    vol_ref, feat_ref,
    ev_ref, w1_ref, wm_ref, b1_ref, bm_ref, rows_ref, wts_ref,
    win, wrecv, x1, x2, x3, t1, t2, t3, bias, fblk, frx, fown, fpart, fback, macc, msend, mrecv, mval, volf, featf, wide, tab,
    in_sem, s1_send, s1_recv, f_send, f_recv, o_send, o_recv, m_send, m_recv, seam_send, far_sem,
):
    cam = lax.axis_index("cam")
    me = lax.axis_index("row")
    odd = lax.rem(cam, 2)
    far = (lax.rem(cam + cams - 1 + 2 * odd, cams), me)
    near = (cam + 1 - 2 * odd, me)
    pair_of = lax.div(me, 2)
    side = lax.rem(me, 2)

    def row_at(dy, dx):
        return 2 * lax.rem(pair_of + dy, BANDS // 2) + lax.rem(side + dx, 2)

    peers = [row_at(dy, dx) for dy, dx in ((2, 1), (2, 0), (1, 1), (3, 1), (1, 0), (3, 0), (0, 1))]

    barrier = pltpu.get_barrier_semaphore()
    for peer in peers:
        pl.semaphore_signal(barrier, inc=1, device_id=(cam, peer), device_id_type=MESH)
    pl.semaphore_signal(barrier, inc=1, device_id=near, device_id_type=MESH)

    place_in_run = lax.rem(cam, cams // 2)
    late = place_in_run == cams // 2 - 1
    early = place_in_run == 0

    @pl.when(jnp.logical_not(late))
    def _():
        pl.semaphore_signal(barrier, inc=1, device_id=far, device_id_type=MESH)

    @pl.when(early)
    def _():
        for peer in peers:
            pl.semaphore_signal(barrier, inc=1, device_id=(far[0], peer), device_id_type=MESH)

    loads = [
        pltpu.make_async_copy(src, dst, in_sem.at[n])
        for n, (src, dst) in enumerate(
            (
                (ev_hbm, ev_ref), (w1_hbm, w1_ref), (wm_hbm, wm_ref), (b1_hbm, b1_ref),
                (bm_hbm, bm_ref), (rows_hbm, rows_ref), (wts_hbm, wts_ref),
            )
        )
    ]
    for load in loads:
        load.start()
    loads[0].wait()

    ev = jnp.dot(row_major_perm(), ev_ref[...], preferred_element_type=F32)
    tiles = [ev[:, LANES * t : LANES * (t + 1)].astype(BF16) for t in range(TILES)]
    for strip in range(BANDS):
        win[strip] = pack_window(window_of(tiles, strip))

    expected = BANDS + 1 + (BANDS - 1) * late.astype(jnp.int32) - early.astype(jnp.int32)
    pl.semaphore_wait(barrier, expected)

    def s1_copy(dst, src_row):
        return pltpu.make_async_remote_copy(
            src_ref=win.at[dst],
            dst_ref=wrecv.at[src_row],
            send_sem=s1_send.at[dst],
            recv_sem=s1_recv.at[src_row],
            device_id=(cam, dst),
            device_id_type=MESH,
        )

    for peer in peers:
        s1_copy(peer, me).start()
    wrecv[me] = win[me]

    @pl.when(late)
    def _():
        pl.semaphore_signal(far_sem, inc=1, device_id=far, device_id_type=MESH)


    for load in loads[1:]:
        load.wait()

    zero_edge = jnp.zeros((EDGE, LANES), BF16)
    for x in (x1, x2, x3):
        for dx in range(5):
            x[dx, 0:EDGE] = zero_edge
            x[dx, EDGE + BANDS * BLK :] = zero_edge
    build_taps(lambda dy, dx: w1_ref[dy, dx], t1)
    build_taps(lambda dy, dx: wm_ref[0, dy, dx], t2)
    build_taps(lambda dy, dx: wm_ref[1, dy, dx], t3)
    perm = channel_major_perm()
    for dx in range(5):
        cols = slice(KROWS * dx, KROWS * (dx + 1))
        t3[:, cols] = jnp.dot(perm, t3[:, cols], preferred_element_type=F32).astype(BF16)
    bias[0] = bias_column(b1_ref[...], False)
    bias[1] = bias_column(bm_ref[0:1], False)
    bias[2] = bias_column(bm_ref[1:2], True)
    for d in range(2):
        edge = jnp.zeros((GROUPS * PACK, ROWS, LANES), F32)
        fpart[d, :, 0:ROWS] = edge
        fpart[d, :, ROWS * (BANDS + 1) :] = edge
    fown[:, 0:ROWS] = edge
    fown[:, ROWS * (BANDS + 1) :] = edge

    first = me * ROWS
    shape = (ROWS, LANES)
    pick = (
        ((row_ids((PLANES * ROWS, 4 * LANES)) & 7) * 64 + (row_ids((PLANES * ROWS, 4 * LANES)) >> 3))
        == lane_ids((PLANES * ROWS, 4 * LANES))
    ).astype(BF16)
    serving = first + row_ids((ROWS, PLANES)) - REACH
    for kind in range(2):
        parts = []
        d = odd if kind == 0 else 1 - odd
        for o in range(SPAN):
            total = jnp.zeros((ROWS, PLANES), F32)
            for k in range(4):
                hit = rows_ref[d, :, k] == serving + o
                total = total + jnp.where(hit, wts_ref[d, :, k], 0.0)
            total = total * (1.0 / CH)
            doubled = jnp.concatenate([total, jnp.zeros((ROWS, 64 - PLANES), F32)], axis=1)
            doubled = jnp.concatenate([doubled, doubled], axis=1)
            half = lane_ids(shape) >> 6
            parts.append(
                jnp.concatenate(
                    [jnp.where(row_ids(shape) == 2 * j + half, doubled, 0.0) for j in range(4)], axis=1
                )
            )
        table = jnp.concatenate(parts, axis=0)
        high = table.astype(BF16).astype(F32)
        table = jnp.concatenate([high, table - high], axis=0).astype(BF16)
        tab[kind] = lax.dot_general(
            pick, table, (((1,), (1,)), ((), ())), preferred_element_type=F32
        ).astype(BF16)

    column = lane_ids((1, LANES)) + me * STRIP - HALO
    inside = jnp.logical_and(column >= 0, column < COLS)

    def put(x, b, value):
        for dx in range(5):
            x[dx, pl.ds(pl.multiple_of(EDGE + BLK * b, EDGE), BLK)] = roll(value, 2 - dx)

    def conv(x, t, pair):
        halves = [
            jnp.concatenate([x[dx, pl.ds(pl.multiple_of(BLK * b, BLK), KROWS)] for dx in range(5)], axis=0)
            for b in (2 * pair, 2 * pair + 1)
        ]
        return jnp.dot(t[...], jnp.concatenate(halves, axis=1), preferred_element_type=F32)

    def hidden(x, t, number, y, pair):
        out = conv(x, t, pair)
        for h in range(2):
            value = jnp.maximum(out[:, LANES * h : LANES * (h + 1)] + bias[number], 0.0)
            put(y, 2 * pair + h, jnp.where(inside, value, 0.0).astype(BF16))

    def f_copy(kind, b):
        return pltpu.make_async_remote_copy(
            src_ref=fblk.at[b],
            dst_ref=frx.at[kind, b],
            send_sem=f_send.at[kind, b],
            recv_sem=f_recv.at[kind, b],
            device_id=far if kind == 0 else near,
            device_id_type=MESH,
        )

    def o_copy(dst, strip):
        return pltpu.make_async_remote_copy(
            src_ref=fblk.at[dst],
            dst_ref=fback.at[strip],
            send_sem=o_send.at[dst],
            recv_sem=o_recv.at[strip],
            device_id=(cam, dst),
            device_id_type=MESH,
        )

    def last(pair):
        out = conv(x3, t3, pair)
        for h in range(2):
            b = 2 * pair + h
            value = out[:, LANES * h : LANES * (h + 1)] + bias[2]
            packed = jnp.concatenate(pack_features(value.reshape(CH, ROWS, LANES)), axis=0)
            packed = packed.astype(BF16)
            fblk[b] = packed
            fown[:, ROWS * (b + 1) : ROWS * (b + 2)] = packed.astype(F32).reshape(
                GROUPS * PACK, ROWS, LANES
            )

        @pl.when(jnp.logical_not(late))
        def _():
            for h in range(2):
                f_copy(0, 2 * pair + h).start()

        for h in range(2):
            f_copy(1, 2 * pair + h).start()

    def take(r):
        s1_copy(peers[0], r).wait_recv()
        put(x1, r, unpack_window(wrecv[r]))

    pairs = BANDS // 2
    put(x1, me, unpack_window(wrecv[me]))
    for dy, dx in ((0, 1), (1, 0), (3, 0), (1, 1), (3, 1)):
        take(row_at(dy, dx))
    hidden(x1, t1, 0, x2, pair_of)
    for dx in range(2):
        take(row_at(2, dx))
    for k in range(1, pairs):
        hidden(x1, t1, 0, x2, lax.rem(pair_of + k, pairs))

    @pl.when(early)
    def _():
        pl.semaphore_wait(far_sem, 1)

    for pair in range(pairs + 1):
        if pair < pairs:
            hidden(x2, t2, 1, x3, pair)
        if pair > 0:
            last(pair - 1)

    fback[me] = fblk[me]

    def m_copy(kind, dst, strip):
        return pltpu.make_async_remote_copy(
            src_ref=msend.at[kind, dst],
            dst_ref=mrecv.at[kind, strip],
            send_sem=m_send.at[kind, dst],
            recv_sem=m_recv.at[kind, strip],
            device_id=(cam, dst),
            device_id_type=MESH,
        )

    def arrive(kind, b):
        f_copy(kind, b).wait_recv()
        fpart[kind, :, ROWS * (b + 1) : ROWS * (b + 2)] = (
            frx[kind, b].astype(F32).reshape(GROUPS * PACK, ROWS, LANES)
        )

    def match(own_ref, part_ref, b):
        def products(n, acc):
            own = own_ref[n, ROWS * (b + 1) : ROWS * (b + 2)]
            return tuple(
                acc[o] + own * part_ref[n, ROWS * (b + 1) + o - REACH : ROWS * (b + 2) + o - REACH]
                for o in range(SPAN)
            )

        def group(g, accs):
            main, tail = accs
            for k in range(4):
                main = products(PACK * g + k, main)
            return main, products(PACK * g + 4, tail)

        zeros = tuple(jnp.zeros((ROWS, LANES), F32) for _ in range(SPAN))
        accs = lax.fori_loop(0, GROUPS, group, (zeros, zeros), unroll=True)
        for n in range(2):
            for o in range(SPAN):
                macc[n, o, ROWS * b : ROWS * (b + 1)] = accs[n][o]

    def finish(kind, first):
        count = ROWS * BANDS // 2
        rows = slice(ROWS * first, ROWS * first + count)
        lane = lane_ids((count, LANES))
        main = [macc[0, o, rows] for o in range(SPAN)]
        tail = [macc[1, o, rows] for o in range(SPAN)]
        out = [fold(lane, 64, main[2 * k], main[2 * k + 1]) for k in range(4)]
        ends = [fold(lane, 64, tail[o], tail[o + 4]) for o in range(4)]
        ends = [fold(lane, 32, ends[o], ends[o + 2]) for o in range(2)]
        out.append(fold(lane, 16, ends[0], ends[1]))
        last_tail = tail[8]
        for step in (64, 32, 16):
            last_tail = last_tail + roll(last_tail, step)
        out.append(jnp.where(lane < 64, main[8] + roll(main[8], 64), last_tail))
        for n in range(BANDS // 2):
            part = [v[ROWS * n : ROWS * (n + 1)] for v in out]
            msend[kind, first + n] = jnp.concatenate(part, axis=0).astype(BF16)

    def seam_copy(dst):
        return pltpu.make_async_remote_copy(
            src_ref=msend.at[2, dst],
            dst_ref=mrecv.at[0, me],
            send_sem=seam_send.at[dst],
            recv_sem=m_recv.at[0, me],
            device_id=(far[0], dst),
            device_id_type=MESH,
        )

    @pl.when(late)
    def _():
        for b in range(BANDS):
            arrive(0, b)
        for first_block in (0, BANDS // 2):
            for b in range(first_block, first_block + BANDS // 2):
                match(fpart.at[0], fown, b)
            finish(2, first_block)
            for dst in range(first_block, first_block + BANDS // 2):
                seam_copy(dst).start()

    for peer in peers:
        o_copy(peer, me).start()

    arrive(1, 0)
    for b in range(BANDS):
        if b + 1 < BANDS:
            arrive(1, b + 1)
        match(fown, fpart.at[1], b)
    for first_block in (0, BANDS // 2):
        finish(1, first_block)
    for peer in peers:
        m_copy(1, peer, me).start()
    mrecv[1, me] = msend[1, me]

    @pl.when(jnp.logical_not(early))
    def _():
        @pl.when(jnp.logical_not(late))
        def _():
            for b in range(BANDS):
                arrive(0, b)

        for b in range(BANDS):
            match(fown, fpart.at[0], b)
        for first_block in (0, BANDS // 2):
            finish(0, first_block)
        for peer in peers:
            m_copy(0, peer, me).start()
        mrecv[0, me] = msend[0, me]

    for k in range(1, BANDS):
        o_copy(peers[0], lax.rem(me + BANDS - k, BANDS)).wait_recv()
    for c in range(CH):
        g, k, h = c >> 3, (c & 7) >> 1, c & 1
        body = (PACK * g + k) * ROWS
        ends = (PACK * g + 4) * ROWS
        end_lane = 16 * k if h else 64 + 16 * k
        pieces = []
        for s in range(BANDS):
            pieces.append((lambda s=s: wide[s, body : body + ROWS], 64 * h, STRIP * s, 64))
            pieces.append((lambda s=s: wide[s, ends : ends + ROWS], end_lane, STRIP * s + 64, 16))
        if c == 0:
            for s in range(BANDS):
                wide[s] = fback[s].astype(F32)
        for t in range(TILES):
            featf[ROWS * c : ROWS * (c + 1), LANES * t : LANES * (t + 1)] = place(pieces, t)
    feat_ref[...] = featf[...].astype(BF16)

    for kind in (1, 0):
        if kind == 0:

            @pl.when(early)
            def _():
                m_copy(0, peers[0], me).wait_recv()

        for k in range(1, BANDS):
            m_copy(kind, peers[0], lax.rem(me + BANDS - k, BANDS)).wait_recv()
        for s in range(BANDS):
            wide[s, 0:MPACK] = mrecv[kind, s].astype(F32)
        for o in range(SPAN):
            body = 8 * (o >> 1) if o < 8 else 5 * ROWS
            body_lane = 64 * (o & 1) if o < 8 else 0
            ends = 4 * ROWS if o < 8 else 5 * ROWS
            end_lane = 16 * o if o < 8 else 64
            pieces = []
            for s in range(BANDS):
                pieces.append((lambda s=s: wide[s, body : body + ROWS], body_lane, STRIP * s, 64))
                pieces.append((lambda s=s: wide[s, ends : ends + ROWS], end_lane, STRIP * s + 64, 16))
            start = ROWS * o
            for t in range(TILES):
                mval[start : start + ROWS, LANES * t : LANES * (t + 1)] = place(pieces, t)
        values = mval[...]
        values = jnp.concatenate([values, values], axis=0).astype(BF16)
        out = jnp.dot(tab[kind], values, preferred_element_type=F32)
        if kind == 1:
            volf[...] = out
        else:
            vol_ref[...] = (volf[...] + out).astype(BF16)

    for peer in peers:
        s1_copy(peer, me).wait_send()
        o_copy(peer, me).wait_send()
        m_copy(1, peer, me).wait_send()
    for b in range(BANDS):
        f_copy(1, b).wait_send()

    @pl.when(jnp.logical_not(early))
    def _():
        for peer in peers:
            m_copy(0, peer, me).wait_send()

    @pl.when(late)
    def _():
        for dst in range(BANDS):
            seam_copy(dst).wait_send()

    @pl.when(jnp.logical_not(late))
    def _():
        for b in range(BANDS):
            f_copy(0, b).wait_send()


def store(vol, feat, vol_out, feat_out, sem):
    copies = [
        pltpu.make_async_copy(vol, vol_out, sem.at[0]),
        pltpu.make_async_copy(feat, feat_out, sem.at[1]),
    ]
    for copy in copies:
        copy.start()
    for copy in copies:
        copy.wait()


def local(cams, events, conv_in, bias_in, conv_mid, bias_mid, tap_rows, tap_weights):
    dma = pltpu.SemaphoreType.DMA
    vmem = pl.BlockSpec(memory_space=pltpu.VMEM)
    padded = (5, BANDS * BLK + 2 * EDGE, LANES)
    taps = (BLK, 5 * KROWS)
    operands = (
        events.reshape(BLK, COLS),
        conv_in.transpose(2, 3, 0, 1),
        conv_mid.transpose(0, 3, 4, 1, 2),
        bias_in.reshape(1, CH),
        bias_mid,
        tap_rows.transpose(0, 2, 3, 1),
        tap_weights.transpose(0, 2, 3, 1),
    )
    vol, feat = pl.pallas_call(
        functools.partial(kernel, cams),
        out_shape=(
            pltpu.VMEM((PLANES * ROWS, COLS), BF16),
            pltpu.VMEM((BLK, COLS), BF16),
        ),
        in_specs=[pl.BlockSpec(memory_space=pltpu.HBM)] * 7,
        out_specs=(vmem, vmem),
        scratch_shapes=[
            *[pltpu.VMEM(operand.shape, operand.dtype) for operand in operands],
            pltpu.VMEM((BANDS, WROWS, LANES), BF16),
            pltpu.VMEM((BANDS, WROWS, LANES), BF16),
            pltpu.VMEM(padded, BF16),
            pltpu.VMEM(padded, BF16),
            pltpu.VMEM(padded, BF16),
            pltpu.VMEM(taps, BF16),
            pltpu.VMEM(taps, BF16),
            pltpu.VMEM(taps, BF16),
            pltpu.VMEM((3, BLK, LANES), F32),
            pltpu.VMEM((BANDS, FROWS, LANES), BF16),
            pltpu.VMEM((2, BANDS, FROWS, LANES), BF16),
            pltpu.VMEM((GROUPS * PACK, ROWS * (BANDS + 2), LANES), F32),
            pltpu.VMEM((2, GROUPS * PACK, ROWS * (BANDS + 2), LANES), F32),
            pltpu.VMEM((BANDS, FROWS, LANES), BF16),
            pltpu.VMEM((2, SPAN, ROWS * BANDS, LANES), F32),
            pltpu.VMEM((3, BANDS, MPACK, LANES), BF16),
            pltpu.VMEM((2, BANDS, MPACK, LANES), BF16),
            pltpu.VMEM((MROWS, COLS), F32),
            pltpu.VMEM((PLANES * ROWS, COLS), F32),
            pltpu.VMEM((BLK, COLS), F32),
            pltpu.VMEM((BANDS, FROWS, LANES), F32),
            pltpu.VMEM((2, PLANES * ROWS, 2 * MROWS), BF16),
            dma((7,)),
            dma((BANDS,)), dma((BANDS,)),
            dma((2, BANDS)), dma((2, BANDS)),
            dma((BANDS,)), dma((BANDS,)),
            dma((2, BANDS)), dma((2, BANDS)),
            dma((BANDS,)), pltpu.SemaphoreType.REGULAR,
        ],
        compiler_params=pltpu.CompilerParams(
            collective_id=0, has_side_effects=True, vmem_limit_bytes=48 * 1024 * 1024
        ),
    )(*[pltpu.with_memory_space_constraint(operand, pltpu.HBM) for operand in operands])
    hbm = pl.BlockSpec(memory_space=pltpu.HBM)
    vol, feat = pl.pallas_call(
        store,
        out_shape=(pltpu.HBM(vol.shape, BF16), pltpu.HBM(feat.shape, BF16)),
        in_specs=[vmem, vmem],
        out_specs=(hbm, hbm),
        scratch_shapes=[dma((2,))],
    )(*[pltpu.with_memory_space_constraint(value, pltpu.VMEM) for value in (vol, feat)])
    return vol.reshape(1, PLANES, ROWS, COLS), feat.reshape(1, CH, ROWS, COLS)


def solution(mesh):
    in_specs = (
        P("cam", None, "row", None),
        P(),
        P(),
        P(),
        P(),
        P(None, None, "row", None),
        P(None, None, "row", None),
    )
    out_specs = (P("cam", None, "row", None), P("cam", None, "row", None))
    return jax.shard_map(
        functools.partial(local, mesh.shape["cam"]),
        mesh=mesh,
        in_specs=in_specs,
        out_specs=out_specs,
        check_vma=False,
    )
```

```python
import functools

import jax
import jax.numpy as jnp
from jax import lax
from jax.experimental import pallas as pl
from jax.experimental.pallas import tpu as pltpu
from jax.sharding import PartitionSpec as P

MESH = pl.DeviceIdType.MESH
F32 = jnp.float32
BF16 = jnp.bfloat16

CH = 32
BANDS = 8
ROWS = 8
COLS = 640
STRIP = COLS // BANDS
HALO = 6
LANES = 128
TILES = COLS // LANES
BLK = CH * ROWS
EDGE = 2 * CH
GROUP = 4
GBLK = GROUP * CH
KROWS = GBLK + 2 * EDGE
PLANES = 48
SPAN = 9
REACH = 4
MROWS = SPAN * ROWS
GROUPS = 4
PACK = 5
FROWS = GROUPS * PACK * ROWS
MPACK = 6 * ROWS
QUARTER = BLK // 4
WROWS = 3 * QUARTER


def lane_ids(shape):
    return lax.broadcasted_iota(jnp.int32, shape, 1)


def row_ids(shape):
    return lax.broadcasted_iota(jnp.int32, shape, 0)


def roll(value, shift):
    shift = shift % value.shape[1]
    return value if shift == 0 else pltpu.roll(value, shift, 1)


def row_major_perm():
    shape = (BLK, BLK)
    i, j = row_ids(shape), lane_ids(shape)
    return ((i & 31) * ROWS + (i >> 5) == j).astype(BF16)


def channel_major_perm():
    shape = (GBLK, GBLK)
    i, j = row_ids(shape), lane_ids(shape)
    return ((i & 3) * CH + (i >> 2) == j).astype(BF16)


def window_of(tiles, strip):
    start = STRIP * strip - HALO
    first = start // LANES
    off = start - first * LANES
    shape = tiles[0].shape
    low = roll(tiles[first], -off) if first >= 0 else jnp.zeros(shape, BF16)
    if LANES - off >= STRIP + 2 * HALO:
        return low
    high = roll(tiles[first + 1], -off) if first + 1 < TILES else jnp.zeros(shape, BF16)
    return jnp.where(lane_ids(shape) < LANES - off, low, high)


def pack_window(value):
    lane = lane_ids((QUARTER, LANES))
    parts = [value[QUARTER * g : QUARTER * (g + 1)] for g in range(4)]
    pairs = [jnp.where(lane < 64, parts[g], roll(parts[g + 1], 64)) for g in (0, 2)]
    tail = roll(parts[0], -64)
    for g in range(1, 4):
        tail = jnp.where(lane >= 32 * g, roll(parts[g], 32 * g - 64), tail)
    return jnp.concatenate(pairs + [tail], axis=0)


def unpack_window(packed):
    lane = lane_ids((QUARTER, LANES))
    tail = packed[2 * QUARTER :]
    parts = []
    for g in range(4):
        pair = packed[QUARTER * (g // 2) : QUARTER * (g // 2 + 1)]
        parts.append(jnp.where(lane < 64, roll(pair, 64 * (g & 1)), roll(tail, 64 - 32 * g)))
    return jnp.concatenate(parts, axis=0)


def fold(lane, step, even, odd):
    clear = (lane & step) == 0
    own = jnp.where(clear, even, odd)
    other = jnp.where(clear, odd, even)
    if step == 64:
        return own + roll(other, 64)
    return own + jnp.where(clear, roll(other, -step), roll(other, step))


def place(pieces, tile):
    out = None
    for get, lane, column, count in pieces:
        lo = max(column, LANES * tile) - LANES * tile
        hi = min(column + count, LANES * (tile + 1)) - LANES * tile
        if lo < hi:
            value = roll(get(), column - LANES * tile - lane)
            out = value if out is None else jnp.where(lane_ids(value.shape) >= lo, value, out)
    return out


def pack_features(upper, lower):
    upper = upper.reshape(CH // 2, ROWS, LANES)
    lower = lower.reshape(CH // 2, ROWS, LANES)
    first = lax.broadcasted_iota(jnp.int32, upper.shape, 1) < GROUP
    evens = jnp.where(first, upper, pltpu.roll(lower, GROUP, 1))
    odds = jnp.where(first, pltpu.roll(upper, GROUP, 1), lower)
    lane = lane_ids((ROWS, LANES))
    out = []
    for g in range(GROUPS):
        tail = None
        for k in range(4):
            even = roll(evens[4 * g + k], -HALO)
            odd = roll(odds[4 * g + k], 64 - HALO)
            out.append(jnp.where(lane < 64, even, odd))
            both = roll(jnp.where(lane < 64, odd, even), 16 * k)
            tail = both if tail is None else jnp.where((lane & 63) >= 16 * k, both, tail)
        out.append(tail)
    return out


def build_taps(w, t_ref):
    for dx in range(5):
        pieces = [w(dy, dx).astype(F32) for dy in range(5)]
        base = jnp.concatenate(pieces + [jnp.zeros((CH, KROWS - 5 * CH), F32)], axis=1)
        for y in range(GROUP):
            t_ref[CH * y : CH * (y + 1), KROWS * dx : KROWS * (dx + 1)] = roll(base, CH * y).astype(BF16)


def bias_column(bias_row, channel_major):
    shape = (GBLK, CH)
    i = row_ids(shape)
    owner = (i >> 2) if channel_major else (i & 31)
    spread = jnp.where(owner == lane_ids(shape), jnp.broadcast_to(bias_row, shape), 0.0)
    return jnp.broadcast_to(jnp.sum(spread, axis=1, keepdims=True), (GBLK, LANES))


def kernel(
    cams,
    ev_hbm, w1_hbm, wm_hbm, b1_hbm, bm_hbm, rows_hbm, wts_hbm,
    vol_ref, feat_ref,
    ev_ref, w1_ref, wm_ref, b1_ref, bm_ref, rows_ref, wts_ref,
    win, wrecv, x1, x2, x3, t1, t2, t3, bias, fblk, frx, fown, fpart, fback, macc, msend, mrecv, mval, volf, featf, wide, tab,
    in_sem, s1_send, s1_recv, f_send, f_recv, o_send, o_recv, m_send, m_recv, seam_send, far_sem,
):
    cam = lax.axis_index("cam")
    me = lax.axis_index("row")
    odd = lax.rem(cam, 2)
    far = (lax.rem(cam + cams - 1 + 2 * odd, cams), me)
    near = (cam + 1 - 2 * odd, me)
    pair_of = lax.div(me, 2)
    side = lax.rem(me, 2)

    def row_at(dy, dx):
        return 2 * lax.rem(pair_of + dy, BANDS // 2) + lax.rem(side + dx, 2)

    peers = [row_at(dy, dx) for dy, dx in ((2, 1), (2, 0), (1, 1), (3, 1), (1, 0), (3, 0), (0, 1))]

    barrier = pltpu.get_barrier_semaphore()
    for peer in peers:
        pl.semaphore_signal(barrier, inc=1, device_id=(cam, peer), device_id_type=MESH)
    pl.semaphore_signal(barrier, inc=1, device_id=near, device_id_type=MESH)

    place_in_run = lax.rem(cam, cams // 2)
    late = place_in_run == cams // 2 - 1
    early = place_in_run == 0

    @pl.when(jnp.logical_not(late))
    def _():
        pl.semaphore_signal(barrier, inc=1, device_id=far, device_id_type=MESH)

    @pl.when(early)
    def _():
        for peer in peers:
            pl.semaphore_signal(barrier, inc=1, device_id=(far[0], peer), device_id_type=MESH)

    loads = [
        pltpu.make_async_copy(src, dst, in_sem.at[n])
        for n, (src, dst) in enumerate(
            (
                (ev_hbm, ev_ref), (w1_hbm, w1_ref), (wm_hbm, wm_ref), (b1_hbm, b1_ref),
                (bm_hbm, bm_ref), (rows_hbm, rows_ref), (wts_hbm, wts_ref),
            )
        )
    ]
    for load in loads:
        load.start()
    loads[0].wait()

    ev = jnp.dot(row_major_perm(), ev_ref[...], preferred_element_type=F32)
    tiles = [ev[:, LANES * t : LANES * (t + 1)].astype(BF16) for t in range(TILES)]
    for strip in range(BANDS):
        win[strip] = pack_window(window_of(tiles, strip))

    expected = BANDS + 1 + (BANDS - 1) * late.astype(jnp.int32) - early.astype(jnp.int32)
    pl.semaphore_wait(barrier, expected)

    def s1_copy(dst, src_row):
        return pltpu.make_async_remote_copy(
            src_ref=win.at[dst],
            dst_ref=wrecv.at[src_row],
            send_sem=s1_send.at[dst],
            recv_sem=s1_recv.at[src_row],
            device_id=(cam, dst),
            device_id_type=MESH,
        )

    for peer in peers:
        s1_copy(peer, me).start()
    wrecv[me] = win[me]

    @pl.when(late)
    def _():
        pl.semaphore_signal(far_sem, inc=1, device_id=far, device_id_type=MESH)


    for load in loads[1:]:
        load.wait()

    zero_edge = jnp.zeros((EDGE, LANES), BF16)
    for x in (x1, x2, x3):
        for dx in range(5):
            x[dx, 0:EDGE] = zero_edge
            x[dx, EDGE + BANDS * BLK :] = zero_edge
    build_taps(lambda dy, dx: w1_ref[dy, dx], t1)
    build_taps(lambda dy, dx: wm_ref[0, dy, dx], t2)
    build_taps(lambda dy, dx: wm_ref[1, dy, dx], t3)
    perm = channel_major_perm()
    for dx in range(5):
        cols = slice(KROWS * dx, KROWS * (dx + 1))
        t3[:, cols] = jnp.dot(perm, t3[:, cols], preferred_element_type=F32).astype(BF16)
    bias[0] = bias_column(b1_ref[...], False)
    bias[1] = bias_column(bm_ref[0:1], False)
    bias[2] = bias_column(bm_ref[1:2], True)
    for d in range(2):
        edge = jnp.zeros((GROUPS * PACK, ROWS, LANES), F32)
        fpart[d, :, 0:ROWS] = edge
        fpart[d, :, ROWS * (BANDS + 1) :] = edge
    fown[:, 0:ROWS] = edge
    fown[:, ROWS * (BANDS + 1) :] = edge

    first = me * ROWS
    shape = (ROWS, LANES)
    pick = (
        ((row_ids((PLANES * ROWS, 4 * LANES)) & 7) * 64 + (row_ids((PLANES * ROWS, 4 * LANES)) >> 3))
        == lane_ids((PLANES * ROWS, 4 * LANES))
    ).astype(BF16)
    serving = first + row_ids((ROWS, PLANES)) - REACH
    for kind in range(2):
        parts = []
        d = odd if kind == 0 else 1 - odd
        for o in range(SPAN):
            total = jnp.zeros((ROWS, PLANES), F32)
            for k in range(4):
                hit = rows_ref[d, :, k] == serving + o
                total = total + jnp.where(hit, wts_ref[d, :, k], 0.0)
            total = total * (1.0 / CH)
            doubled = jnp.concatenate([total, jnp.zeros((ROWS, 64 - PLANES), F32)], axis=1)
            doubled = jnp.concatenate([doubled, doubled], axis=1)
            half = lane_ids(shape) >> 6
            parts.append(
                jnp.concatenate(
                    [jnp.where(row_ids(shape) == 2 * j + half, doubled, 0.0) for j in range(4)], axis=1
                )
            )
        table = jnp.concatenate(parts, axis=0)
        high = table.astype(BF16).astype(F32)
        table = jnp.concatenate([high, table - high], axis=0).astype(BF16)
        tab[kind] = lax.dot_general(
            pick, table, (((1,), (1,)), ((), ())), preferred_element_type=F32
        ).astype(BF16)

    column = lane_ids((1, LANES)) + me * STRIP - HALO
    inside = jnp.logical_and(column >= 0, column < COLS)

    def put(x, start, value):
        start = pl.multiple_of(EDGE + start, EDGE)
        for dx in range(5):
            x[dx, pl.ds(start, value.shape[0])] = roll(value, 2 - dx)

    def conv(x, t, pair):
        out = []
        for half in range(2):
            cols = [
                jnp.concatenate([x[dx, GBLK * g : GBLK * g + KROWS] for dx in range(5)], axis=0)
                for g in (4 * pair + 2 * half, 4 * pair + 2 * half + 1)
            ]
            both = jnp.dot(t[...], jnp.concatenate(cols, axis=1), preferred_element_type=F32)
            out += [both[:, :LANES], both[:, LANES:]]
        return out

    def hidden(x, t, number, y, pair):
        for n, out in enumerate(conv(x, t, pair)):
            value = jnp.maximum(out + bias[number], 0.0)
            put(y, GBLK * (4 * pair + n), jnp.where(inside, value, 0.0).astype(BF16))

    def f_copy(kind, b):
        return pltpu.make_async_remote_copy(
            src_ref=fblk.at[b],
            dst_ref=frx.at[kind, b],
            send_sem=f_send.at[kind, b],
            recv_sem=f_recv.at[kind, b],
            device_id=far if kind == 0 else near,
            device_id_type=MESH,
        )

    def o_copy(dst, strip):
        return pltpu.make_async_remote_copy(
            src_ref=fblk.at[dst],
            dst_ref=fback.at[strip],
            send_sem=o_send.at[dst],
            recv_sem=o_recv.at[strip],
            device_id=(cam, dst),
            device_id_type=MESH,
        )

    def last(pair):
        out = conv(x3, t3, pair)
        for h in range(2):
            b = 2 * pair + h
            packed = pack_features(out[2 * h] + bias[2], out[2 * h + 1] + bias[2])
            packed = jnp.concatenate(packed, axis=0)
            packed = packed.astype(BF16)
            fblk[b] = packed
            fown[:, ROWS * (b + 1) : ROWS * (b + 2)] = packed.astype(F32).reshape(
                GROUPS * PACK, ROWS, LANES
            )

        @pl.when(jnp.logical_not(late))
        def _():
            for h in range(2):
                f_copy(0, 2 * pair + h).start()
            for h in range(2):

                @pl.when(me != 2 * pair + h)
                def _(b=2 * pair + h):
                    o_copy(b, me).start()

        for h in range(2):
            f_copy(1, 2 * pair + h).start()

    def take(r):
        s1_copy(peers[0], r).wait_recv()
        put(x1, BLK * r, unpack_window(wrecv[r]))

    put(x1, BLK * me, unpack_window(wrecv[me]))
    for peer in reversed(peers):
        take(peer)

    pairs = BANDS // 2
    for step in range(pairs + 2):
        if step < pairs:
            hidden(x1, t1, 0, x2, step)
        if 0 <= step - 1 < pairs:
            hidden(x2, t2, 1, x3, step - 1)
        if step == 2:

            @pl.when(early)
            def _():
                pl.semaphore_wait(far_sem, 1)

        if 0 <= step - 2 < pairs:
            last(step - 2)

    fback[me] = fblk[me]

    def m_copy(kind, dst, strip):
        return pltpu.make_async_remote_copy(
            src_ref=msend.at[kind, dst],
            dst_ref=mrecv.at[kind, strip],
            send_sem=m_send.at[kind, dst],
            recv_sem=m_recv.at[kind, strip],
            device_id=(cam, dst),
            device_id_type=MESH,
        )

    def arrive(kind, b):
        f_copy(kind, b).wait_recv()
        fpart[kind, :, ROWS * (b + 1) : ROWS * (b + 2)] = (
            frx[kind, b].astype(F32).reshape(GROUPS * PACK, ROWS, LANES)
        )

    def match(own_ref, part_ref, b):
        def products(n, acc):
            own = own_ref[n, ROWS * (b + 1) : ROWS * (b + 2)]
            return tuple(
                acc[o] + own * part_ref[n, ROWS * (b + 1) + o - REACH : ROWS * (b + 2) + o - REACH]
                for o in range(SPAN)
            )

        def group(g, accs):
            main, tail = accs
            for k in range(4):
                main = products(PACK * g + k, main)
            return main, products(PACK * g + 4, tail)

        zeros = tuple(jnp.zeros((ROWS, LANES), F32) for _ in range(SPAN))
        accs = lax.fori_loop(0, GROUPS, group, (zeros, zeros), unroll=True)
        for n in range(2):
            for o in range(SPAN):
                macc[n, o, ROWS * b : ROWS * (b + 1)] = accs[n][o]

    def finish(kind, first):
        count = ROWS * BANDS // 2
        rows = slice(ROWS * first, ROWS * first + count)
        lane = lane_ids((count, LANES))
        main = [macc[0, o, rows] for o in range(SPAN)]
        tail = [macc[1, o, rows] for o in range(SPAN)]
        out = [fold(lane, 64, main[2 * k], main[2 * k + 1]) for k in range(4)]
        ends = [fold(lane, 64, tail[o], tail[o + 4]) for o in range(4)]
        ends = [fold(lane, 32, ends[o], ends[o + 2]) for o in range(2)]
        out.append(fold(lane, 16, ends[0], ends[1]))
        last_tail = tail[8]
        for step in (64, 32, 16):
            last_tail = last_tail + roll(last_tail, step)
        out.append(jnp.where(lane < 64, main[8] + roll(main[8], 64), last_tail))
        for n in range(BANDS // 2):
            part = [v[ROWS * n : ROWS * (n + 1)] for v in out]
            msend[kind, first + n] = jnp.concatenate(part, axis=0).astype(BF16)

    def seam_copy(dst):
        return pltpu.make_async_remote_copy(
            src_ref=msend.at[2, dst],
            dst_ref=mrecv.at[0, me],
            send_sem=seam_send.at[dst],
            recv_sem=m_recv.at[0, me],
            device_id=(far[0], dst),
            device_id_type=MESH,
        )

    @pl.when(late)
    def _():
        for b in range(BANDS):
            arrive(0, b)
        for first_block in (0, BANDS // 2):
            for b in range(first_block, first_block + BANDS // 2):
                match(fpart.at[0], fown, b)
            finish(2, first_block)
            for dst in range(first_block, first_block + BANDS // 2):
                seam_copy(dst).start()

        for peer in peers:
            o_copy(peer, me).start()

    arrive(1, 0)
    for b in range(BANDS):
        if b + 1 < BANDS:
            arrive(1, b + 1)
        match(fown, fpart.at[1], b)
    for first_block in (0, BANDS // 2):
        finish(1, first_block)
    for peer in peers:
        m_copy(1, peer, me).start()
    mrecv[1, me] = msend[1, me]

    @pl.when(jnp.logical_not(early))
    def _():
        @pl.when(jnp.logical_not(late))
        def _():
            for b in range(BANDS):
                arrive(0, b)

        for b in range(BANDS):
            match(fown, fpart.at[0], b)
        for first_block in (0, BANDS // 2):
            finish(0, first_block)
        for peer in peers:
            m_copy(0, peer, me).start()
        mrecv[0, me] = msend[0, me]

    for k in range(1, BANDS):
        o_copy(peers[0], lax.rem(me + BANDS - k, BANDS)).wait_recv()
    for c in range(CH):
        g, k, h = c >> 3, (c & 7) >> 1, c & 1
        body = (PACK * g + k) * ROWS
        ends = (PACK * g + 4) * ROWS
        end_lane = 16 * k if h else 64 + 16 * k
        pieces = []
        for s in range(BANDS):
            pieces.append((lambda s=s: wide[s, body : body + ROWS], 64 * h, STRIP * s, 64))
            pieces.append((lambda s=s: wide[s, ends : ends + ROWS], end_lane, STRIP * s + 64, 16))
        if c == 0:
            for s in range(BANDS):
                wide[s] = fback[s].astype(F32)
        for t in range(TILES):
            featf[ROWS * c : ROWS * (c + 1), LANES * t : LANES * (t + 1)] = place(pieces, t)
    feat_ref[...] = featf[...].astype(BF16)

    for kind in (1, 0):
        if kind == 0:

            @pl.when(early)
            def _():
                m_copy(0, peers[0], me).wait_recv()

        for k in range(1, BANDS):
            m_copy(kind, peers[0], lax.rem(me + BANDS - k, BANDS)).wait_recv()
        for s in range(BANDS):
            wide[s, 0:MPACK] = mrecv[kind, s].astype(F32)
        for o in range(SPAN):
            body = 8 * (o >> 1) if o < 8 else 5 * ROWS
            body_lane = 64 * (o & 1) if o < 8 else 0
            ends = 4 * ROWS if o < 8 else 5 * ROWS
            end_lane = 16 * o if o < 8 else 64
            pieces = []
            for s in range(BANDS):
                pieces.append((lambda s=s: wide[s, body : body + ROWS], body_lane, STRIP * s, 64))
                pieces.append((lambda s=s: wide[s, ends : ends + ROWS], end_lane, STRIP * s + 64, 16))
            start = ROWS * o
            for t in range(TILES):
                mval[start : start + ROWS, LANES * t : LANES * (t + 1)] = place(pieces, t)
        values = mval[...]
        values = jnp.concatenate([values, values], axis=0).astype(BF16)
        out = jnp.dot(tab[kind], values, preferred_element_type=F32)
        if kind == 1:
            volf[...] = out
        else:
            vol_ref[...] = (volf[...] + out).astype(BF16)

    for peer in peers:
        s1_copy(peer, me).wait_send()
        o_copy(peer, me).wait_send()
        m_copy(1, peer, me).wait_send()
    for b in range(BANDS):
        f_copy(1, b).wait_send()

    @pl.when(jnp.logical_not(early))
    def _():
        for peer in peers:
            m_copy(0, peer, me).wait_send()

    @pl.when(late)
    def _():
        for dst in range(BANDS):
            seam_copy(dst).wait_send()

    @pl.when(jnp.logical_not(late))
    def _():
        for b in range(BANDS):
            f_copy(0, b).wait_send()


def store(vol, feat, vol_out, feat_out, sem):
    copies = [
        pltpu.make_async_copy(vol, vol_out, sem.at[0]),
        pltpu.make_async_copy(feat, feat_out, sem.at[1]),
    ]
    for copy in copies:
        copy.start()
    for copy in copies:
        copy.wait()


def local(cams, events, conv_in, bias_in, conv_mid, bias_mid, tap_rows, tap_weights):
    dma = pltpu.SemaphoreType.DMA
    vmem = pl.BlockSpec(memory_space=pltpu.VMEM)
    padded = (5, BANDS * BLK + 2 * EDGE, LANES)
    taps = (GBLK, 5 * KROWS)
    operands = (
        events.reshape(BLK, COLS),
        conv_in.transpose(2, 3, 0, 1),
        conv_mid.transpose(0, 3, 4, 1, 2),
        bias_in.reshape(1, CH),
        bias_mid,
        tap_rows.transpose(0, 2, 3, 1),
        tap_weights.transpose(0, 2, 3, 1),
    )
    vol, feat = pl.pallas_call(
        functools.partial(kernel, cams),
        out_shape=(
            pltpu.VMEM((PLANES * ROWS, COLS), BF16),
            pltpu.VMEM((BLK, COLS), BF16),
        ),
        in_specs=[pl.BlockSpec(memory_space=pltpu.HBM)] * 7,
        out_specs=(vmem, vmem),
        scratch_shapes=[
            *[pltpu.VMEM(operand.shape, operand.dtype) for operand in operands],
            pltpu.VMEM((BANDS, WROWS, LANES), BF16),
            pltpu.VMEM((BANDS, WROWS, LANES), BF16),
            pltpu.VMEM(padded, BF16),
            pltpu.VMEM(padded, BF16),
            pltpu.VMEM(padded, BF16),
            pltpu.VMEM(taps, BF16),
            pltpu.VMEM(taps, BF16),
            pltpu.VMEM(taps, BF16),
            pltpu.VMEM((3, GBLK, LANES), F32),
            pltpu.VMEM((BANDS, FROWS, LANES), BF16),
            pltpu.VMEM((2, BANDS, FROWS, LANES), BF16),
            pltpu.VMEM((GROUPS * PACK, ROWS * (BANDS + 2), LANES), F32),
            pltpu.VMEM((2, GROUPS * PACK, ROWS * (BANDS + 2), LANES), F32),
            pltpu.VMEM((BANDS, FROWS, LANES), BF16),
            pltpu.VMEM((2, SPAN, ROWS * BANDS, LANES), F32),
            pltpu.VMEM((3, BANDS, MPACK, LANES), BF16),
            pltpu.VMEM((2, BANDS, MPACK, LANES), BF16),
            pltpu.VMEM((MROWS, COLS), F32),
            pltpu.VMEM((PLANES * ROWS, COLS), F32),
            pltpu.VMEM((BLK, COLS), F32),
            pltpu.VMEM((BANDS, FROWS, LANES), F32),
            pltpu.VMEM((2, PLANES * ROWS, 2 * MROWS), BF16),
            dma((7,)),
            dma((BANDS,)), dma((BANDS,)),
            dma((2, BANDS)), dma((2, BANDS)),
            dma((BANDS,)), dma((BANDS,)),
            dma((2, BANDS)), dma((2, BANDS)),
            dma((BANDS,)), pltpu.SemaphoreType.REGULAR,
        ],
        compiler_params=pltpu.CompilerParams(
            collective_id=0, has_side_effects=True, vmem_limit_bytes=48 * 1024 * 1024
        ),
    )(*[pltpu.with_memory_space_constraint(operand, pltpu.HBM) for operand in operands])
    hbm = pl.BlockSpec(memory_space=pltpu.HBM)
    vol, feat = pl.pallas_call(
        store,
        out_shape=(pltpu.HBM(vol.shape, BF16), pltpu.HBM(feat.shape, BF16)),
        in_specs=[vmem, vmem],
        out_specs=(hbm, hbm),
        scratch_shapes=[dma((2,))],
    )(*[pltpu.with_memory_space_constraint(value, pltpu.VMEM) for value in (vol, feat)])
    return vol.reshape(1, PLANES, ROWS, COLS), feat.reshape(1, CH, ROWS, COLS)


def solution(mesh):
    in_specs = (
        P("cam", None, "row", None),
        P(),
        P(),
        P(),
        P(),
        P(None, None, "row", None),
        P(None, None, "row", None),
    )
    out_specs = (P("cam", None, "row", None), P("cam", None, "row", None))
    return jax.shard_map(
        functools.partial(local, mesh.shape["cam"]),
        mesh=mesh,
        in_specs=in_specs,
        out_specs=out_specs,
        check_vma=False,
    )
```

```python
import functools

import jax
import jax.numpy as jnp
from jax import lax
from jax.experimental import pallas as pl
from jax.experimental.pallas import tpu as pltpu
from jax.sharding import PartitionSpec as P

MESH = pl.DeviceIdType.MESH
F32 = jnp.float32
BF16 = jnp.bfloat16

CH = 32
BANDS = 8
ROWS = 8
COLS = 640
STRIP = COLS // BANDS
HALO = 6
LANES = 128
TILES = COLS // LANES
BLK = CH * ROWS
EDGE = 2 * CH
GROUP = 4
GBLK = GROUP * CH
KROWS = GBLK + 2 * EDGE
PLANES = 48
SPAN = 9
REACH = 4
MROWS = SPAN * ROWS
GROUPS = 4
PACK = 5
FROWS = GROUPS * PACK * ROWS
MPACK = 6 * ROWS
QUARTER = BLK // 4
WROWS = 3 * QUARTER


def lane_ids(shape):
    return lax.broadcasted_iota(jnp.int32, shape, 1)


def row_ids(shape):
    return lax.broadcasted_iota(jnp.int32, shape, 0)


def roll(value, shift):
    shift = shift % value.shape[1]
    return value if shift == 0 else pltpu.roll(value, shift, 1)


def row_major_perm():
    shape = (BLK, BLK)
    i, j = row_ids(shape), lane_ids(shape)
    return ((i & 31) * ROWS + (i >> 5) == j).astype(BF16)


def channel_major_perm():
    shape = (GBLK, GBLK)
    i, j = row_ids(shape), lane_ids(shape)
    return ((i & 3) * CH + (i >> 2) == j).astype(BF16)


def window_of(tiles, strip):
    start = STRIP * strip - HALO
    first = start // LANES
    off = start - first * LANES
    shape = tiles[0].shape
    low = roll(tiles[first], -off) if first >= 0 else jnp.zeros(shape, BF16)
    if LANES - off >= STRIP + 2 * HALO:
        return low
    high = roll(tiles[first + 1], -off) if first + 1 < TILES else jnp.zeros(shape, BF16)
    return jnp.where(lane_ids(shape) < LANES - off, low, high)


def pack_window(value):
    lane = lane_ids((QUARTER, LANES))
    parts = [value[QUARTER * g : QUARTER * (g + 1)] for g in range(4)]
    pairs = [jnp.where(lane < 64, parts[g], roll(parts[g + 1], 64)) for g in (0, 2)]
    tail = roll(parts[0], -64)
    for g in range(1, 4):
        tail = jnp.where(lane >= 32 * g, roll(parts[g], 32 * g - 64), tail)
    return jnp.concatenate(pairs + [tail], axis=0)


def unpack_window(packed):
    lane = lane_ids((QUARTER, LANES))
    tail = packed[2 * QUARTER :]
    parts = []
    for g in range(4):
        pair = packed[QUARTER * (g // 2) : QUARTER * (g // 2 + 1)]
        parts.append(jnp.where(lane < 64, roll(pair, 64 * (g & 1)), roll(tail, 64 - 32 * g)))
    return jnp.concatenate(parts, axis=0)


def fold(lane, step, even, odd):
    clear = (lane & step) == 0
    own = jnp.where(clear, even, odd)
    other = jnp.where(clear, odd, even)
    if step == 64:
        return own + roll(other, 64)
    return own + jnp.where(clear, roll(other, -step), roll(other, step))


def place(pieces, tile):
    out = None
    for get, lane, column, count in pieces:
        lo = max(column, LANES * tile) - LANES * tile
        hi = min(column + count, LANES * (tile + 1)) - LANES * tile
        if lo < hi:
            value = roll(get(), column - LANES * tile - lane)
            out = value if out is None else jnp.where(lane_ids(value.shape) >= lo, value, out)
    return out


def pack_features(upper, lower):
    upper = upper.reshape(CH // 2, ROWS, LANES)
    lower = lower.reshape(CH // 2, ROWS, LANES)
    first = lax.broadcasted_iota(jnp.int32, upper.shape, 1) < GROUP
    evens = jnp.where(first, upper, pltpu.roll(lower, GROUP, 1))
    odds = jnp.where(first, pltpu.roll(upper, GROUP, 1), lower)
    lane = lane_ids((ROWS, LANES))
    out = []
    for g in range(GROUPS):
        tail = None
        for k in range(4):
            even = roll(evens[4 * g + k], -HALO)
            odd = roll(odds[4 * g + k], 64 - HALO)
            out.append(jnp.where(lane < 64, even, odd))
            both = roll(jnp.where(lane < 64, odd, even), 16 * k)
            tail = both if tail is None else jnp.where((lane & 63) >= 16 * k, both, tail)
        out.append(tail)
    return out


def build_taps(w, t_ref):
    for dx in range(5):
        pieces = [w(dy, dx).astype(F32) for dy in range(5)]
        base = jnp.concatenate(pieces + [jnp.zeros((CH, KROWS - 5 * CH), F32)], axis=1)
        for y in range(GROUP):
            t_ref[CH * y : CH * (y + 1), KROWS * dx : KROWS * (dx + 1)] = roll(base, CH * y).astype(BF16)


def bias_column(bias_row, channel_major):
    shape = (GBLK, CH)
    i = row_ids(shape)
    owner = (i >> 2) if channel_major else (i & 31)
    spread = jnp.where(owner == lane_ids(shape), jnp.broadcast_to(bias_row, shape), 0.0)
    return jnp.broadcast_to(jnp.sum(spread, axis=1, keepdims=True), (GBLK, LANES))


def kernel(
    cams,
    ev_hbm, w1_hbm, wm_hbm, b1_hbm, bm_hbm, rows_hbm, wts_hbm,
    vol_ref, feat_ref,
    ev_ref, w1_ref, wm_ref, b1_ref, bm_ref, rows_ref, wts_ref,
    win, wrecv, x1, x2, x3, t1, t2, t3, bias, fblk, frx, fown, fpart, fback, macc, msend, mrecv, mval, volf, featf, wide, tab,
    in_sem, s1_send, s1_recv, f_send, f_recv, o_send, o_recv, m_send, m_recv, seam_send, far_sem,
):
    cam = lax.axis_index("cam")
    me = lax.axis_index("row")
    odd = lax.rem(cam, 2)
    far = (lax.rem(cam + cams - 1 + 2 * odd, cams), me)
    near = (cam + 1 - 2 * odd, me)
    pair_of = lax.div(me, 2)
    side = lax.rem(me, 2)

    def row_at(dy, dx):
        return 2 * lax.rem(pair_of + dy, BANDS // 2) + lax.rem(side + dx, 2)

    peers = [row_at(dy, dx) for dy, dx in ((2, 1), (2, 0), (1, 1), (3, 1), (1, 0), (3, 0), (0, 1))]

    barrier = pltpu.get_barrier_semaphore()
    for peer in peers:
        pl.semaphore_signal(barrier, inc=1, device_id=(cam, peer), device_id_type=MESH)
    pl.semaphore_signal(barrier, inc=1, device_id=near, device_id_type=MESH)

    place_in_run = lax.rem(cam, cams // 2)
    late = place_in_run == cams // 2 - 1
    early = place_in_run == 0
    defer = jnp.logical_or(place_in_run < 2, place_in_run >= cams // 2 - 2)

    @pl.when(jnp.logical_not(late))
    def _():
        pl.semaphore_signal(barrier, inc=1, device_id=far, device_id_type=MESH)

    @pl.when(early)
    def _():
        for peer in peers:
            pl.semaphore_signal(barrier, inc=1, device_id=(far[0], peer), device_id_type=MESH)

    loads = [
        pltpu.make_async_copy(src, dst, in_sem.at[n])
        for n, (src, dst) in enumerate(
            (
                (ev_hbm, ev_ref), (w1_hbm, w1_ref), (wm_hbm, wm_ref), (b1_hbm, b1_ref),
                (bm_hbm, bm_ref), (rows_hbm, rows_ref), (wts_hbm, wts_ref),
            )
        )
    ]
    for load in loads:
        load.start()
    loads[0].wait()

    ev = jnp.dot(row_major_perm(), ev_ref[...], preferred_element_type=F32)
    tiles = [ev[:, LANES * t : LANES * (t + 1)].astype(BF16) for t in range(TILES)]
    for strip in range(BANDS):
        win[strip] = pack_window(window_of(tiles, strip))

    expected = BANDS + 1 + (BANDS - 1) * late.astype(jnp.int32) - early.astype(jnp.int32)
    pl.semaphore_wait(barrier, expected)

    def s1_copy(dst, src_row):
        return pltpu.make_async_remote_copy(
            src_ref=win.at[dst],
            dst_ref=wrecv.at[src_row],
            send_sem=s1_send.at[dst],
            recv_sem=s1_recv.at[src_row],
            device_id=(cam, dst),
            device_id_type=MESH,
        )

    for peer in peers:
        s1_copy(peer, me).start()
    wrecv[me] = win[me]

    @pl.when(late)
    def _():
        pl.semaphore_signal(far_sem, inc=1, device_id=far, device_id_type=MESH)


    for load in loads[1:]:
        load.wait()

    zero_edge = jnp.zeros((EDGE, LANES), BF16)
    for x in (x1, x2, x3):
        for dx in range(5):
            x[dx, 0:EDGE] = zero_edge
            x[dx, EDGE + BANDS * BLK :] = zero_edge
    build_taps(lambda dy, dx: w1_ref[dy, dx], t1)
    build_taps(lambda dy, dx: wm_ref[0, dy, dx], t2)
    build_taps(lambda dy, dx: wm_ref[1, dy, dx], t3)
    perm = channel_major_perm()
    for dx in range(5):
        cols = slice(KROWS * dx, KROWS * (dx + 1))
        t3[:, cols] = jnp.dot(perm, t3[:, cols], preferred_element_type=F32).astype(BF16)
    bias[0] = bias_column(b1_ref[...], False)
    bias[1] = bias_column(bm_ref[0:1], False)
    bias[2] = bias_column(bm_ref[1:2], True)
    for d in range(2):
        edge = jnp.zeros((GROUPS * PACK, ROWS, LANES), F32)
        fpart[d, :, 0:ROWS] = edge
        fpart[d, :, ROWS * (BANDS + 1) :] = edge
    fown[:, 0:ROWS] = edge
    fown[:, ROWS * (BANDS + 1) :] = edge

    first = me * ROWS
    shape = (ROWS, LANES)
    pick = (
        ((row_ids((PLANES * ROWS, 4 * LANES)) & 7) * 64 + (row_ids((PLANES * ROWS, 4 * LANES)) >> 3))
        == lane_ids((PLANES * ROWS, 4 * LANES))
    ).astype(BF16)
    serving = first + row_ids((ROWS, PLANES)) - REACH
    for kind in range(2):
        parts = []
        d = odd if kind == 0 else 1 - odd
        for o in range(SPAN):
            total = jnp.zeros((ROWS, PLANES), F32)
            for k in range(4):
                hit = rows_ref[d, :, k] == serving + o
                total = total + jnp.where(hit, wts_ref[d, :, k], 0.0)
            total = total * (1.0 / CH)
            doubled = jnp.concatenate([total, jnp.zeros((ROWS, 64 - PLANES), F32)], axis=1)
            doubled = jnp.concatenate([doubled, doubled], axis=1)
            half = lane_ids(shape) >> 6
            parts.append(
                jnp.concatenate(
                    [jnp.where(row_ids(shape) == 2 * j + half, doubled, 0.0) for j in range(4)], axis=1
                )
            )
        table = jnp.concatenate(parts, axis=0)
        high = table.astype(BF16).astype(F32)
        table = jnp.concatenate([high, table - high], axis=0).astype(BF16)
        tab[kind] = lax.dot_general(
            pick, table, (((1,), (1,)), ((), ())), preferred_element_type=F32
        ).astype(BF16)

    column = lane_ids((1, LANES)) + me * STRIP - HALO
    inside = jnp.logical_and(column >= 0, column < COLS)

    def put(x, start, value):
        start = pl.multiple_of(EDGE + start, EDGE)
        for dx in range(5):
            x[dx, pl.ds(start, value.shape[0])] = roll(value, 2 - dx)

    def conv(x, t, pair):
        out = []
        for half in range(2):
            cols = [
                jnp.concatenate([x[dx, GBLK * g : GBLK * g + KROWS] for dx in range(5)], axis=0)
                for g in (4 * pair + 2 * half, 4 * pair + 2 * half + 1)
            ]
            both = jnp.dot(t[...], jnp.concatenate(cols, axis=1), preferred_element_type=F32)
            out += [both[:, :LANES], both[:, LANES:]]
        return out

    def hidden(x, t, number, y, pair):
        for n, out in enumerate(conv(x, t, pair)):
            value = jnp.maximum(out + bias[number], 0.0)
            put(y, GBLK * (4 * pair + n), jnp.where(inside, value, 0.0).astype(BF16))

    def f_copy(kind, b):
        return pltpu.make_async_remote_copy(
            src_ref=fblk.at[b],
            dst_ref=frx.at[kind, b],
            send_sem=f_send.at[kind, b],
            recv_sem=f_recv.at[kind, b],
            device_id=far if kind == 0 else near,
            device_id_type=MESH,
        )

    def o_copy(dst, strip):
        return pltpu.make_async_remote_copy(
            src_ref=fblk.at[dst],
            dst_ref=fback.at[strip],
            send_sem=o_send.at[dst],
            recv_sem=o_recv.at[strip],
            device_id=(cam, dst),
            device_id_type=MESH,
        )

    def last(pair):
        out = conv(x3, t3, pair)
        for h in range(2):
            b = 2 * pair + h
            packed = pack_features(out[2 * h] + bias[2], out[2 * h + 1] + bias[2])
            packed = jnp.concatenate(packed, axis=0)
            packed = packed.astype(BF16)
            fblk[b] = packed
            fown[:, ROWS * (b + 1) : ROWS * (b + 2)] = packed.astype(F32).reshape(
                GROUPS * PACK, ROWS, LANES
            )

        @pl.when(jnp.logical_not(late))
        def _():
            for h in range(2):
                f_copy(0, 2 * pair + h).start()

        @pl.when(jnp.logical_not(defer))
        def _():
            for h in range(2):

                @pl.when(me != 2 * pair + h)
                def _(b=2 * pair + h):
                    o_copy(b, me).start()

        for h in range(2):
            f_copy(1, 2 * pair + h).start()

    def take(r):
        s1_copy(peers[0], r).wait_recv()
        put(x1, BLK * r, unpack_window(wrecv[r]))

    put(x1, BLK * me, unpack_window(wrecv[me]))
    for peer in reversed(peers):
        take(peer)

    pairs = BANDS // 2
    for step in range(pairs + 2):
        if step < pairs:
            hidden(x1, t1, 0, x2, step)
        if 0 <= step - 1 < pairs:
            hidden(x2, t2, 1, x3, step - 1)
        if step == 2:

            @pl.when(early)
            def _():
                pl.semaphore_wait(far_sem, 1)

        if 0 <= step - 2 < pairs:
            last(step - 2)

    fback[me] = fblk[me]

    def m_copy(kind, dst, strip):
        return pltpu.make_async_remote_copy(
            src_ref=msend.at[kind, dst],
            dst_ref=mrecv.at[kind, strip],
            send_sem=m_send.at[kind, dst],
            recv_sem=m_recv.at[kind, strip],
            device_id=(cam, dst),
            device_id_type=MESH,
        )

    def arrive(kind, b):
        f_copy(kind, b).wait_recv()
        fpart[kind, :, ROWS * (b + 1) : ROWS * (b + 2)] = (
            frx[kind, b].astype(F32).reshape(GROUPS * PACK, ROWS, LANES)
        )

    def match(own_ref, part_ref, b):
        def products(n, acc):
            own = own_ref[n, ROWS * (b + 1) : ROWS * (b + 2)]
            return tuple(
                acc[o] + own * part_ref[n, ROWS * (b + 1) + o - REACH : ROWS * (b + 2) + o - REACH]
                for o in range(SPAN)
            )

        def group(g, accs):
            main, tail = accs
            for k in range(4):
                main = products(PACK * g + k, main)
            return main, products(PACK * g + 4, tail)

        zeros = tuple(jnp.zeros((ROWS, LANES), F32) for _ in range(SPAN))
        accs = lax.fori_loop(0, GROUPS, group, (zeros, zeros), unroll=True)
        for n in range(2):
            for o in range(SPAN):
                macc[n, o, ROWS * b : ROWS * (b + 1)] = accs[n][o]

    def finish(kind, first):
        count = ROWS * BANDS // 2
        rows = slice(ROWS * first, ROWS * first + count)
        lane = lane_ids((count, LANES))
        main = [macc[0, o, rows] for o in range(SPAN)]
        tail = [macc[1, o, rows] for o in range(SPAN)]
        out = [fold(lane, 64, main[2 * k], main[2 * k + 1]) for k in range(4)]
        ends = [fold(lane, 64, tail[o], tail[o + 4]) for o in range(4)]
        ends = [fold(lane, 32, ends[o], ends[o + 2]) for o in range(2)]
        out.append(fold(lane, 16, ends[0], ends[1]))
        last_tail = tail[8]
        for step in (64, 32, 16):
            last_tail = last_tail + roll(last_tail, step)
        out.append(jnp.where(lane < 64, main[8] + roll(main[8], 64), last_tail))
        for n in range(BANDS // 2):
            part = [v[ROWS * n : ROWS * (n + 1)] for v in out]
            msend[kind, first + n] = jnp.concatenate(part, axis=0).astype(BF16)

    def seam_copy(dst):
        return pltpu.make_async_remote_copy(
            src_ref=msend.at[2, dst],
            dst_ref=mrecv.at[0, me],
            send_sem=seam_send.at[dst],
            recv_sem=m_recv.at[0, me],
            device_id=(far[0], dst),
            device_id_type=MESH,
        )

    @pl.when(late)
    def _():
        for b in range(BANDS):
            arrive(0, b)
        for first_block in (0, BANDS // 2):
            for b in range(first_block, first_block + BANDS // 2):
                match(fpart.at[0], fown, b)
            finish(2, first_block)
            for dst in range(first_block, first_block + BANDS // 2):
                seam_copy(dst).start()

    @pl.when(defer)
    def _():
        for peer in peers:
            o_copy(peer, me).start()

    arrive(1, 0)
    for b in range(BANDS):
        if b + 1 < BANDS:
            arrive(1, b + 1)
        match(fown, fpart.at[1], b)
    for first_block in (0, BANDS // 2):
        finish(1, first_block)
    for peer in peers:
        m_copy(1, peer, me).start()
    mrecv[1, me] = msend[1, me]

    @pl.when(jnp.logical_not(early))
    def _():
        @pl.when(jnp.logical_not(late))
        def _():
            for b in range(BANDS):
                arrive(0, b)

        for b in range(BANDS):
            match(fown, fpart.at[0], b)
        for first_block in (0, BANDS // 2):
            finish(0, first_block)
        for peer in peers:
            m_copy(0, peer, me).start()
        mrecv[0, me] = msend[0, me]

    for k in range(1, BANDS):
        o_copy(peers[0], lax.rem(me + BANDS - k, BANDS)).wait_recv()
    for c in range(CH):
        g, k, h = c >> 3, (c & 7) >> 1, c & 1
        body = (PACK * g + k) * ROWS
        ends = (PACK * g + 4) * ROWS
        end_lane = 16 * k if h else 64 + 16 * k
        pieces = []
        for s in range(BANDS):
            pieces.append((lambda s=s: wide[s, body : body + ROWS], 64 * h, STRIP * s, 64))
            pieces.append((lambda s=s: wide[s, ends : ends + ROWS], end_lane, STRIP * s + 64, 16))
        if c == 0:
            for s in range(BANDS):
                wide[s] = fback[s].astype(F32)
        for t in range(TILES):
            featf[ROWS * c : ROWS * (c + 1), LANES * t : LANES * (t + 1)] = place(pieces, t)
    feat_ref[...] = featf[...].astype(BF16)

    for kind in (1, 0):
        if kind == 0:

            @pl.when(early)
            def _():
                m_copy(0, peers[0], me).wait_recv()

        for k in range(1, BANDS):
            m_copy(kind, peers[0], lax.rem(me + BANDS - k, BANDS)).wait_recv()
        for s in range(BANDS):
            wide[s, 0:MPACK] = mrecv[kind, s].astype(F32)
        for o in range(SPAN):
            body = 8 * (o >> 1) if o < 8 else 5 * ROWS
            body_lane = 64 * (o & 1) if o < 8 else 0
            ends = 4 * ROWS if o < 8 else 5 * ROWS
            end_lane = 16 * o if o < 8 else 64
            pieces = []
            for s in range(BANDS):
                pieces.append((lambda s=s: wide[s, body : body + ROWS], body_lane, STRIP * s, 64))
                pieces.append((lambda s=s: wide[s, ends : ends + ROWS], end_lane, STRIP * s + 64, 16))
            start = ROWS * o
            for t in range(TILES):
                mval[start : start + ROWS, LANES * t : LANES * (t + 1)] = place(pieces, t)
        values = mval[...]
        values = jnp.concatenate([values, values], axis=0).astype(BF16)
        out = jnp.dot(tab[kind], values, preferred_element_type=F32)
        if kind == 1:
            volf[...] = out
        else:
            vol_ref[...] = (volf[...] + out).astype(BF16)

    for peer in peers:
        s1_copy(peer, me).wait_send()
        o_copy(peer, me).wait_send()
        m_copy(1, peer, me).wait_send()
    for b in range(BANDS):
        f_copy(1, b).wait_send()

    @pl.when(jnp.logical_not(early))
    def _():
        for peer in peers:
            m_copy(0, peer, me).wait_send()

    @pl.when(late)
    def _():
        for dst in range(BANDS):
            seam_copy(dst).wait_send()

    @pl.when(jnp.logical_not(late))
    def _():
        for b in range(BANDS):
            f_copy(0, b).wait_send()


def store(vol, feat, vol_out, feat_out, sem):
    copies = [
        pltpu.make_async_copy(vol, vol_out, sem.at[0]),
        pltpu.make_async_copy(feat, feat_out, sem.at[1]),
    ]
    for copy in copies:
        copy.start()
    for copy in copies:
        copy.wait()


def local(cams, events, conv_in, bias_in, conv_mid, bias_mid, tap_rows, tap_weights):
    dma = pltpu.SemaphoreType.DMA
    vmem = pl.BlockSpec(memory_space=pltpu.VMEM)
    padded = (5, BANDS * BLK + 2 * EDGE, LANES)
    taps = (GBLK, 5 * KROWS)
    operands = (
        events.reshape(BLK, COLS),
        conv_in.transpose(2, 3, 0, 1),
        conv_mid.transpose(0, 3, 4, 1, 2),
        bias_in.reshape(1, CH),
        bias_mid,
        tap_rows.transpose(0, 2, 3, 1),
        tap_weights.transpose(0, 2, 3, 1),
    )
    vol, feat = pl.pallas_call(
        functools.partial(kernel, cams),
        out_shape=(
            pltpu.VMEM((PLANES * ROWS, COLS), BF16),
            pltpu.VMEM((BLK, COLS), BF16),
        ),
        in_specs=[pl.BlockSpec(memory_space=pltpu.HBM)] * 7,
        out_specs=(vmem, vmem),
        scratch_shapes=[
            *[pltpu.VMEM(operand.shape, operand.dtype) for operand in operands],
            pltpu.VMEM((BANDS, WROWS, LANES), BF16),
            pltpu.VMEM((BANDS, WROWS, LANES), BF16),
            pltpu.VMEM(padded, BF16),
            pltpu.VMEM(padded, BF16),
            pltpu.VMEM(padded, BF16),
            pltpu.VMEM(taps, BF16),
            pltpu.VMEM(taps, BF16),
            pltpu.VMEM(taps, BF16),
            pltpu.VMEM((3, GBLK, LANES), F32),
            pltpu.VMEM((BANDS, FROWS, LANES), BF16),
            pltpu.VMEM((2, BANDS, FROWS, LANES), BF16),
            pltpu.VMEM((GROUPS * PACK, ROWS * (BANDS + 2), LANES), F32),
            pltpu.VMEM((2, GROUPS * PACK, ROWS * (BANDS + 2), LANES), F32),
            pltpu.VMEM((BANDS, FROWS, LANES), BF16),
            pltpu.VMEM((2, SPAN, ROWS * BANDS, LANES), F32),
            pltpu.VMEM((3, BANDS, MPACK, LANES), BF16),
            pltpu.VMEM((2, BANDS, MPACK, LANES), BF16),
            pltpu.VMEM((MROWS, COLS), F32),
            pltpu.VMEM((PLANES * ROWS, COLS), F32),
            pltpu.VMEM((BLK, COLS), F32),
            pltpu.VMEM((BANDS, FROWS, LANES), F32),
            pltpu.VMEM((2, PLANES * ROWS, 2 * MROWS), BF16),
            dma((7,)),
            dma((BANDS,)), dma((BANDS,)),
            dma((2, BANDS)), dma((2, BANDS)),
            dma((BANDS,)), dma((BANDS,)),
            dma((2, BANDS)), dma((2, BANDS)),
            dma((BANDS,)), pltpu.SemaphoreType.REGULAR,
        ],
        compiler_params=pltpu.CompilerParams(
            collective_id=0, has_side_effects=True, vmem_limit_bytes=48 * 1024 * 1024
        ),
    )(*[pltpu.with_memory_space_constraint(operand, pltpu.HBM) for operand in operands])
    hbm = pl.BlockSpec(memory_space=pltpu.HBM)
    vol, feat = pl.pallas_call(
        store,
        out_shape=(pltpu.HBM(vol.shape, BF16), pltpu.HBM(feat.shape, BF16)),
        in_specs=[vmem, vmem],
        out_specs=(hbm, hbm),
        scratch_shapes=[dma((2,))],
    )(*[pltpu.with_memory_space_constraint(value, pltpu.VMEM) for value in (vol, feat)])
    return vol.reshape(1, PLANES, ROWS, COLS), feat.reshape(1, CH, ROWS, COLS)


def solution(mesh):
    in_specs = (
        P("cam", None, "row", None),
        P(),
        P(),
        P(),
        P(),
        P(None, None, "row", None),
        P(None, None, "row", None),
    )
    out_specs = (P("cam", None, "row", None), P("cam", None, "row", None))
    return jax.shard_map(
        functools.partial(local, mesh.shape["cam"]),
        mesh=mesh,
        in_specs=in_specs,
        out_specs=out_specs,
        check_vma=False,
    )
```

```python
import functools

import jax
import jax.numpy as jnp
from jax import lax
from jax.experimental import pallas as pl
from jax.experimental.pallas import tpu as pltpu
from jax.sharding import PartitionSpec as P

MESH = pl.DeviceIdType.MESH
F32 = jnp.float32
BF16 = jnp.bfloat16

CH = 32
BANDS = 8
ROWS = 8
COLS = 640
STRIP = COLS // BANDS
HALO = 6
LANES = 128
TILES = COLS // LANES
BLK = CH * ROWS
EDGE = 2 * CH
GROUP = 4
GBLK = GROUP * CH
KROWS = GBLK + 2 * EDGE
PLANES = 48
SPAN = 9
REACH = 4
MROWS = SPAN * ROWS
GROUPS = 4
PACK = 5
FROWS = GROUPS * PACK * ROWS
MPACK = 6 * ROWS
QUARTER = BLK // 4
WROWS = 3 * QUARTER


def lane_ids(shape):
    return lax.broadcasted_iota(jnp.int32, shape, 1)


def row_ids(shape):
    return lax.broadcasted_iota(jnp.int32, shape, 0)


def roll(value, shift):
    shift = shift % value.shape[1]
    return value if shift == 0 else pltpu.roll(value, shift, 1)


def row_major_perm():
    shape = (BLK, BLK)
    i, j = row_ids(shape), lane_ids(shape)
    return ((i & 31) * ROWS + (i >> 5) == j).astype(BF16)


def channel_major_perm():
    shape = (GBLK, GBLK)
    i, j = row_ids(shape), lane_ids(shape)
    return ((i & 3) * CH + (i >> 2) == j).astype(BF16)


def window_of(tiles, strip):
    start = STRIP * strip - HALO
    first = start // LANES
    off = start - first * LANES
    shape = tiles[0].shape
    low = roll(tiles[first], -off) if first >= 0 else jnp.zeros(shape, BF16)
    if LANES - off >= STRIP + 2 * HALO:
        return low
    high = roll(tiles[first + 1], -off) if first + 1 < TILES else jnp.zeros(shape, BF16)
    return jnp.where(lane_ids(shape) < LANES - off, low, high)


def pack_window(value):
    lane = lane_ids((QUARTER, LANES))
    parts = [value[QUARTER * g : QUARTER * (g + 1)] for g in range(4)]
    pairs = [jnp.where(lane < 64, parts[g], roll(parts[g + 1], 64)) for g in (0, 2)]
    tail = roll(parts[0], -64)
    for g in range(1, 4):
        tail = jnp.where(lane >= 32 * g, roll(parts[g], 32 * g - 64), tail)
    return jnp.concatenate(pairs + [tail], axis=0)


def unpack_window(packed):
    lane = lane_ids((QUARTER, LANES))
    tail = packed[2 * QUARTER :]
    parts = []
    for g in range(4):
        pair = packed[QUARTER * (g // 2) : QUARTER * (g // 2 + 1)]
        parts.append(jnp.where(lane < 64, roll(pair, 64 * (g & 1)), roll(tail, 64 - 32 * g)))
    return jnp.concatenate(parts, axis=0)


def fold(lane, step, even, odd):
    clear = (lane & step) == 0
    own = jnp.where(clear, even, odd)
    other = jnp.where(clear, odd, even)
    if step == 64:
        return own + roll(other, 64)
    return own + jnp.where(clear, roll(other, -step), roll(other, step))


def place(pieces, tile):
    out = None
    for get, lane, column, count in pieces:
        lo = max(column, LANES * tile) - LANES * tile
        hi = min(column + count, LANES * (tile + 1)) - LANES * tile
        if lo < hi:
            value = roll(get(), column - LANES * tile - lane)
            out = value if out is None else jnp.where(lane_ids(value.shape) >= lo, value, out)
    return out


def pack_features(upper, lower):
    upper = upper.reshape(CH // 2, ROWS, LANES)
    lower = lower.reshape(CH // 2, ROWS, LANES)
    first = lax.broadcasted_iota(jnp.int32, upper.shape, 1) < GROUP
    evens = jnp.where(first, upper, pltpu.roll(lower, GROUP, 1))
    odds = jnp.where(first, pltpu.roll(upper, GROUP, 1), lower)
    lane = lane_ids((ROWS, LANES))
    out = []
    for g in range(GROUPS):
        tail = None
        for k in range(4):
            even = roll(evens[4 * g + k], -HALO)
            odd = roll(odds[4 * g + k], 64 - HALO)
            out.append(jnp.where(lane < 64, even, odd))
            both = roll(jnp.where(lane < 64, odd, even), 16 * k)
            tail = both if tail is None else jnp.where((lane & 63) >= 16 * k, both, tail)
        out.append(tail)
    return out


def build_taps(w, t_ref):
    for dx in range(5):
        pieces = [w(dy, dx).astype(F32) for dy in range(5)]
        base = jnp.concatenate(pieces + [jnp.zeros((CH, KROWS - 5 * CH), F32)], axis=1)
        for y in range(GROUP):
            t_ref[CH * y : CH * (y + 1), KROWS * dx : KROWS * (dx + 1)] = roll(base, CH * y).astype(BF16)


def bias_column(bias_row, channel_major):
    shape = (GBLK, CH)
    i = row_ids(shape)
    owner = (i >> 2) if channel_major else (i & 31)
    spread = jnp.where(owner == lane_ids(shape), jnp.broadcast_to(bias_row, shape), 0.0)
    return jnp.broadcast_to(jnp.sum(spread, axis=1, keepdims=True), (GBLK, LANES))


def kernel(
    cams,
    ev_hbm, w1_hbm, wm_hbm, b1_hbm, bm_hbm, rows_hbm, wts_hbm,
    vol_ref, feat_ref,
    ev_ref, w1_ref, wm_ref, b1_ref, bm_ref, rows_ref, wts_ref,
    win, wrecv, x1, x2, x3, t1, t2, t3, bias, fblk, frx, fown, fpart, fback, macc, msend, mrecv, mval, volf, featf, wide, tab,
    in_sem, s1_send, s1_recv, f_send, f_recv, o_send, o_recv, m_send, m_recv, seam_send, far_sem,
):
    cam = lax.axis_index("cam")
    me = lax.axis_index("row")
    odd = lax.rem(cam, 2)
    far = (lax.rem(cam + cams - 1 + 2 * odd, cams), me)
    near = (cam + 1 - 2 * odd, me)
    pair_of = lax.div(me, 2)
    side = lax.rem(me, 2)

    def row_at(dy, dx):
        return 2 * lax.rem(pair_of + dy, BANDS // 2) + lax.rem(side + dx, 2)

    peers = [row_at(dy, dx) for dy, dx in ((2, 1), (2, 0), (1, 1), (3, 1), (1, 0), (3, 0), (0, 1))]

    barrier = pltpu.get_barrier_semaphore()
    for peer in peers:
        pl.semaphore_signal(barrier, inc=1, device_id=(cam, peer), device_id_type=MESH)
    pl.semaphore_signal(barrier, inc=1, device_id=near, device_id_type=MESH)

    place_in_run = lax.rem(cam, cams // 2)
    late = place_in_run == cams // 2 - 1
    early = place_in_run == 0

    @pl.when(jnp.logical_not(late))
    def _():
        pl.semaphore_signal(barrier, inc=1, device_id=far, device_id_type=MESH)

    @pl.when(early)
    def _():
        for peer in peers:
            pl.semaphore_signal(barrier, inc=1, device_id=(far[0], peer), device_id_type=MESH)

    loads = [
        pltpu.make_async_copy(src, dst, in_sem.at[n])
        for n, (src, dst) in enumerate(
            (
                (ev_hbm, ev_ref), (w1_hbm, w1_ref), (wm_hbm, wm_ref), (b1_hbm, b1_ref),
                (bm_hbm, bm_ref), (rows_hbm, rows_ref), (wts_hbm, wts_ref),
            )
        )
    ]
    for load in loads:
        load.start()
    loads[0].wait()

    ev = jnp.dot(row_major_perm(), ev_ref[...], preferred_element_type=F32)
    tiles = [ev[:, LANES * t : LANES * (t + 1)].astype(BF16) for t in range(TILES)]
    for strip in range(BANDS):
        win[strip] = pack_window(window_of(tiles, strip))

    expected = BANDS + 1 + (BANDS - 1) * late.astype(jnp.int32) - early.astype(jnp.int32)
    pl.semaphore_wait(barrier, expected)

    def s1_copy(dst, src_row):
        return pltpu.make_async_remote_copy(
            src_ref=win.at[dst],
            dst_ref=wrecv.at[src_row],
            send_sem=s1_send.at[dst],
            recv_sem=s1_recv.at[src_row],
            device_id=(cam, dst),
            device_id_type=MESH,
        )

    for peer in peers:
        s1_copy(peer, me).start()
    wrecv[me] = win[me]

    @pl.when(late)
    def _():
        pl.semaphore_signal(far_sem, inc=1, device_id=far, device_id_type=MESH)


    for load in loads[1:]:
        load.wait()

    zero_edge = jnp.zeros((EDGE, LANES), BF16)
    for x in (x1, x2, x3):
        for dx in range(5):
            x[dx, 0:EDGE] = zero_edge
            x[dx, EDGE + BANDS * BLK :] = zero_edge
    build_taps(lambda dy, dx: w1_ref[dy, dx], t1)
    build_taps(lambda dy, dx: wm_ref[0, dy, dx], t2)
    build_taps(lambda dy, dx: wm_ref[1, dy, dx], t3)
    perm = channel_major_perm()
    for dx in range(5):
        cols = slice(KROWS * dx, KROWS * (dx + 1))
        t3[:, cols] = jnp.dot(perm, t3[:, cols], preferred_element_type=F32).astype(BF16)
    bias[0] = bias_column(b1_ref[...], False)
    bias[1] = bias_column(bm_ref[0:1], False)
    bias[2] = bias_column(bm_ref[1:2], True)
    for d in range(2):
        edge = jnp.zeros((GROUPS * PACK, ROWS, LANES), F32)
        fpart[d, :, 0:ROWS] = edge
        fpart[d, :, ROWS * (BANDS + 1) :] = edge
    fown[:, 0:ROWS] = edge
    fown[:, ROWS * (BANDS + 1) :] = edge

    first = me * ROWS
    shape = (ROWS, LANES)
    pick = (
        ((row_ids((PLANES * ROWS, 4 * LANES)) & 7) * 64 + (row_ids((PLANES * ROWS, 4 * LANES)) >> 3))
        == lane_ids((PLANES * ROWS, 4 * LANES))
    ).astype(BF16)
    serving = first + row_ids((ROWS, PLANES)) - REACH
    for kind in range(2):
        parts = []
        d = odd if kind == 0 else 1 - odd
        for o in range(SPAN):
            total = jnp.zeros((ROWS, PLANES), F32)
            for k in range(4):
                hit = rows_ref[d, :, k] == serving + o
                total = total + jnp.where(hit, wts_ref[d, :, k], 0.0)
            total = total * (1.0 / CH)
            doubled = jnp.concatenate([total, jnp.zeros((ROWS, 64 - PLANES), F32)], axis=1)
            doubled = jnp.concatenate([doubled, doubled], axis=1)
            half = lane_ids(shape) >> 6
            parts.append(
                jnp.concatenate(
                    [jnp.where(row_ids(shape) == 2 * j + half, doubled, 0.0) for j in range(4)], axis=1
                )
            )
        table = jnp.concatenate(parts, axis=0)
        high = table.astype(BF16).astype(F32)
        table = jnp.concatenate([high, table - high], axis=0).astype(BF16)
        tab[kind] = lax.dot_general(
            pick, table, (((1,), (1,)), ((), ())), preferred_element_type=F32
        ).astype(BF16)

    column = lane_ids((1, LANES)) + me * STRIP - HALO
    inside = jnp.logical_and(column >= 0, column < COLS)

    def put(x, start, value):
        start = pl.multiple_of(EDGE + start, EDGE)
        for dx in range(5):
            x[dx, pl.ds(start, value.shape[0])] = roll(value, 2 - dx)

    def conv(x, t, pair):
        out = []
        for half in range(2):
            cols = [
                jnp.concatenate([x[dx, GBLK * g : GBLK * g + KROWS] for dx in range(5)], axis=0)
                for g in (4 * pair + 2 * half, 4 * pair + 2 * half + 1)
            ]
            both = jnp.dot(t[...], jnp.concatenate(cols, axis=1), preferred_element_type=F32)
            out += [both[:, :LANES], both[:, LANES:]]
        return out

    def hidden(x, t, number, y, pair):
        for n, out in enumerate(conv(x, t, pair)):
            value = jnp.maximum(out + bias[number], 0.0)
            put(y, GBLK * (4 * pair + n), jnp.where(inside, value, 0.0).astype(BF16))

    def f_copy(kind, b):
        return pltpu.make_async_remote_copy(
            src_ref=fblk.at[b],
            dst_ref=frx.at[kind, b],
            send_sem=f_send.at[kind, b],
            recv_sem=f_recv.at[kind, b],
            device_id=far if kind == 0 else near,
            device_id_type=MESH,
        )

    def o_copy(dst, strip):
        return pltpu.make_async_remote_copy(
            src_ref=fblk.at[dst],
            dst_ref=fback.at[strip],
            send_sem=o_send.at[dst],
            recv_sem=o_recv.at[strip],
            device_id=(cam, dst),
            device_id_type=MESH,
        )

    def last(pair):
        out = conv(x3, t3, pair)
        for h in range(2):
            b = 2 * pair + h
            packed = pack_features(out[2 * h] + bias[2], out[2 * h + 1] + bias[2])
            packed = jnp.concatenate(packed, axis=0)
            packed = packed.astype(BF16)
            fblk[b] = packed
            fown[:, ROWS * (b + 1) : ROWS * (b + 2)] = packed.astype(F32).reshape(
                GROUPS * PACK, ROWS, LANES
            )

        @pl.when(jnp.logical_not(late))
        def _():
            for h in range(2):
                f_copy(0, 2 * pair + h).start()
            for h in range(2):

                @pl.when(me != 2 * pair + h)
                def _(b=2 * pair + h):
                    o_copy(b, me).start()

        for h in range(2):
            f_copy(1, 2 * pair + h).start()

    def take(r):
        s1_copy(peers[0], r).wait_recv()
        put(x1, BLK * r, unpack_window(wrecv[r]))

    put(x1, BLK * me, unpack_window(wrecv[me]))
    for peer in reversed(peers):
        take(peer)

    pairs = BANDS // 2
    for step in range(pairs + 2):
        if step < pairs:
            hidden(x1, t1, 0, x2, step)
        if 0 <= step - 1 < pairs:
            hidden(x2, t2, 1, x3, step - 1)
        if step == 2:

            @pl.when(early)
            def _():
                pl.semaphore_wait(far_sem, 1)

        if 0 <= step - 2 < pairs:
            last(step - 2)

    fback[me] = fblk[me]

    def m_copy(kind, dst, strip):
        return pltpu.make_async_remote_copy(
            src_ref=msend.at[kind, dst],
            dst_ref=mrecv.at[kind, strip],
            send_sem=m_send.at[kind, dst],
            recv_sem=m_recv.at[kind, strip],
            device_id=(cam, dst),
            device_id_type=MESH,
        )

    def arrive(kind, b):
        f_copy(kind, b).wait_recv()
        fpart[kind, :, ROWS * (b + 1) : ROWS * (b + 2)] = (
            frx[kind, b].astype(F32).reshape(GROUPS * PACK, ROWS, LANES)
        )

    def match(own_ref, part_ref, b):
        def products(n, acc):
            own = own_ref[n, ROWS * (b + 1) : ROWS * (b + 2)]
            return tuple(
                acc[o] + own * part_ref[n, ROWS * (b + 1) + o - REACH : ROWS * (b + 2) + o - REACH]
                for o in range(SPAN)
            )

        def group(g, accs):
            main, tail = accs
            for k in range(4):
                main = products(PACK * g + k, main)
            return main, products(PACK * g + 4, tail)

        zeros = tuple(jnp.zeros((ROWS, LANES), F32) for _ in range(SPAN))
        accs = lax.fori_loop(0, GROUPS, group, (zeros, zeros), unroll=True)
        for n in range(2):
            for o in range(SPAN):
                macc[n, o, ROWS * b : ROWS * (b + 1)] = accs[n][o]

    def finish(kind, first):
        count = ROWS * BANDS // 2
        rows = slice(ROWS * first, ROWS * first + count)
        lane = lane_ids((count, LANES))
        main = [macc[0, o, rows] for o in range(SPAN)]
        tail = [macc[1, o, rows] for o in range(SPAN)]
        out = [fold(lane, 64, main[2 * k], main[2 * k + 1]) for k in range(4)]
        ends = [fold(lane, 64, tail[o], tail[o + 4]) for o in range(4)]
        ends = [fold(lane, 32, ends[o], ends[o + 2]) for o in range(2)]
        out.append(fold(lane, 16, ends[0], ends[1]))
        last_tail = tail[8]
        for step in (64, 32, 16):
            last_tail = last_tail + roll(last_tail, step)
        out.append(jnp.where(lane < 64, main[8] + roll(main[8], 64), last_tail))
        for n in range(BANDS // 2):
            part = [v[ROWS * n : ROWS * (n + 1)] for v in out]
            msend[kind, first + n] = jnp.concatenate(part, axis=0).astype(BF16)

    def seam_copy(dst):
        return pltpu.make_async_remote_copy(
            src_ref=msend.at[2, dst],
            dst_ref=mrecv.at[0, me],
            send_sem=seam_send.at[dst],
            recv_sem=m_recv.at[0, me],
            device_id=(far[0], dst),
            device_id_type=MESH,
        )

    @pl.when(late)
    def _():
        for first_block in (0, BANDS // 2):
            for b in range(first_block, first_block + BANDS // 2):
                arrive(0, b)
                match(fpart.at[0], fown, b)
            finish(2, first_block)
            for dst in range(first_block, first_block + BANDS // 2):
                seam_copy(dst).start()

        for peer in peers:
            o_copy(peer, me).start()

    arrive(1, 0)
    for b in range(BANDS):
        if b + 1 < BANDS:
            arrive(1, b + 1)
        match(fown, fpart.at[1], b)
    for first_block in (0, BANDS // 2):
        finish(1, first_block)
    for peer in peers:
        m_copy(1, peer, me).start()
    mrecv[1, me] = msend[1, me]

    @pl.when(jnp.logical_not(early))
    def _():
        @pl.when(jnp.logical_not(late))
        def _():
            for b in range(BANDS):
                arrive(0, b)

        for b in range(BANDS):
            match(fown, fpart.at[0], b)
        for first_block in (0, BANDS // 2):
            finish(0, first_block)
        for peer in peers:
            m_copy(0, peer, me).start()
        mrecv[0, me] = msend[0, me]

    for k in range(1, BANDS):
        o_copy(peers[0], lax.rem(me + BANDS - k, BANDS)).wait_recv()
    for c in range(CH):
        g, k, h = c >> 3, (c & 7) >> 1, c & 1
        body = (PACK * g + k) * ROWS
        ends = (PACK * g + 4) * ROWS
        end_lane = 16 * k if h else 64 + 16 * k
        pieces = []
        for s in range(BANDS):
            pieces.append((lambda s=s: wide[s, body : body + ROWS], 64 * h, STRIP * s, 64))
            pieces.append((lambda s=s: wide[s, ends : ends + ROWS], end_lane, STRIP * s + 64, 16))
        if c == 0:
            for s in range(BANDS):
                wide[s] = fback[s].astype(F32)
        for t in range(TILES):
            featf[ROWS * c : ROWS * (c + 1), LANES * t : LANES * (t + 1)] = place(pieces, t)
    feat_ref[...] = featf[...].astype(BF16)

    for kind in (1, 0):
        if kind == 0:

            @pl.when(early)
            def _():
                m_copy(0, peers[0], me).wait_recv()

        for k in range(1, BANDS):
            m_copy(kind, peers[0], lax.rem(me + BANDS - k, BANDS)).wait_recv()
        for s in range(BANDS):
            wide[s, 0:MPACK] = mrecv[kind, s].astype(F32)
        for o in range(SPAN):
            body = 8 * (o >> 1) if o < 8 else 5 * ROWS
            body_lane = 64 * (o & 1) if o < 8 else 0
            ends = 4 * ROWS if o < 8 else 5 * ROWS
            end_lane = 16 * o if o < 8 else 64
            pieces = []
            for s in range(BANDS):
                pieces.append((lambda s=s: wide[s, body : body + ROWS], body_lane, STRIP * s, 64))
                pieces.append((lambda s=s: wide[s, ends : ends + ROWS], end_lane, STRIP * s + 64, 16))
            start = ROWS * o
            for t in range(TILES):
                mval[start : start + ROWS, LANES * t : LANES * (t + 1)] = place(pieces, t)
        values = mval[...]
        values = jnp.concatenate([values, values], axis=0).astype(BF16)
        out = jnp.dot(tab[kind], values, preferred_element_type=F32)
        if kind == 1:
            volf[...] = out
        else:
            vol_ref[...] = (volf[...] + out).astype(BF16)

    for peer in peers:
        s1_copy(peer, me).wait_send()
        o_copy(peer, me).wait_send()
        m_copy(1, peer, me).wait_send()
    for b in range(BANDS):
        f_copy(1, b).wait_send()

    @pl.when(jnp.logical_not(early))
    def _():
        for peer in peers:
            m_copy(0, peer, me).wait_send()

    @pl.when(late)
    def _():
        for dst in range(BANDS):
            seam_copy(dst).wait_send()

    @pl.when(jnp.logical_not(late))
    def _():
        for b in range(BANDS):
            f_copy(0, b).wait_send()


def store(vol, feat, vol_out, feat_out, sem):
    copies = [
        pltpu.make_async_copy(vol, vol_out, sem.at[0]),
        pltpu.make_async_copy(feat, feat_out, sem.at[1]),
    ]
    for copy in copies:
        copy.start()
    for copy in copies:
        copy.wait()


def local(cams, events, conv_in, bias_in, conv_mid, bias_mid, tap_rows, tap_weights):
    dma = pltpu.SemaphoreType.DMA
    vmem = pl.BlockSpec(memory_space=pltpu.VMEM)
    padded = (5, BANDS * BLK + 2 * EDGE, LANES)
    taps = (GBLK, 5 * KROWS)
    operands = (
        events.reshape(BLK, COLS),
        conv_in.transpose(2, 3, 0, 1),
        conv_mid.transpose(0, 3, 4, 1, 2),
        bias_in.reshape(1, CH),
        bias_mid,
        tap_rows.transpose(0, 2, 3, 1),
        tap_weights.transpose(0, 2, 3, 1),
    )
    vol, feat = pl.pallas_call(
        functools.partial(kernel, cams),
        out_shape=(
            pltpu.VMEM((PLANES * ROWS, COLS), BF16),
            pltpu.VMEM((BLK, COLS), BF16),
        ),
        in_specs=[pl.BlockSpec(memory_space=pltpu.HBM)] * 7,
        out_specs=(vmem, vmem),
        scratch_shapes=[
            *[pltpu.VMEM(operand.shape, operand.dtype) for operand in operands],
            pltpu.VMEM((BANDS, WROWS, LANES), BF16),
            pltpu.VMEM((BANDS, WROWS, LANES), BF16),
            pltpu.VMEM(padded, BF16),
            pltpu.VMEM(padded, BF16),
            pltpu.VMEM(padded, BF16),
            pltpu.VMEM(taps, BF16),
            pltpu.VMEM(taps, BF16),
            pltpu.VMEM(taps, BF16),
            pltpu.VMEM((3, GBLK, LANES), F32),
            pltpu.VMEM((BANDS, FROWS, LANES), BF16),
            pltpu.VMEM((2, BANDS, FROWS, LANES), BF16),
            pltpu.VMEM((GROUPS * PACK, ROWS * (BANDS + 2), LANES), F32),
            pltpu.VMEM((2, GROUPS * PACK, ROWS * (BANDS + 2), LANES), F32),
            pltpu.VMEM((BANDS, FROWS, LANES), BF16),
            pltpu.VMEM((2, SPAN, ROWS * BANDS, LANES), F32),
            pltpu.VMEM((3, BANDS, MPACK, LANES), BF16),
            pltpu.VMEM((2, BANDS, MPACK, LANES), BF16),
            pltpu.VMEM((MROWS, COLS), F32),
            pltpu.VMEM((PLANES * ROWS, COLS), F32),
            pltpu.VMEM((BLK, COLS), F32),
            pltpu.VMEM((BANDS, FROWS, LANES), F32),
            pltpu.VMEM((2, PLANES * ROWS, 2 * MROWS), BF16),
            dma((7,)),
            dma((BANDS,)), dma((BANDS,)),
            dma((2, BANDS)), dma((2, BANDS)),
            dma((BANDS,)), dma((BANDS,)),
            dma((2, BANDS)), dma((2, BANDS)),
            dma((BANDS,)), pltpu.SemaphoreType.REGULAR,
        ],
        compiler_params=pltpu.CompilerParams(
            collective_id=0, has_side_effects=True, vmem_limit_bytes=48 * 1024 * 1024
        ),
    )(*[pltpu.with_memory_space_constraint(operand, pltpu.HBM) for operand in operands])
    hbm = pl.BlockSpec(memory_space=pltpu.HBM)
    vol, feat = pl.pallas_call(
        store,
        out_shape=(pltpu.HBM(vol.shape, BF16), pltpu.HBM(feat.shape, BF16)),
        in_specs=[vmem, vmem],
        out_specs=(hbm, hbm),
        scratch_shapes=[dma((2,))],
    )(*[pltpu.with_memory_space_constraint(value, pltpu.VMEM) for value in (vol, feat)])
    return vol.reshape(1, PLANES, ROWS, COLS), feat.reshape(1, CH, ROWS, COLS)


def solution(mesh):
    in_specs = (
        P("cam", None, "row", None),
        P(),
        P(),
        P(),
        P(),
        P(None, None, "row", None),
        P(None, None, "row", None),
    )
    out_specs = (P("cam", None, "row", None), P("cam", None, "row", None))
    return jax.shard_map(
        functools.partial(local, mesh.shape["cam"]),
        mesh=mesh,
        in_specs=in_specs,
        out_specs=out_specs,
        check_vma=False,
    )
```
